256 devices in a mesh: orb: 32 (over y, z), slab: 8 (over x, core).
Axes of the slice: x: 4, y: 4, z: 8, core: 2. Of those that a mesh axis runs over, the one named last changes fastest.
Arguments:
- orbitals: float32 [2, 4096, 16384], P(None, 'orb', 'slab'), may hold values from -1.5 to 1.5
- offsets: int32 [4096], replicated, may hold values from 0 to 6080, as said below
- pairs: int32 [32, 3], P('orb'), may hold values from 0 to 1, as said below
- kernel: float32 [32, 3, 128, 128], P('orb'), may hold values from -0.6 to 0.6
Outputs:
- gradient: float32 [4096, 16384], P('orb', 'slab')
The draws below stay inside these ranges and needn't reach their ends.
Inputs may be any that keep to these rules, and one draw needn't show every extreme that they name: offsets[f] lies between 192 * (f // 128) and 192 * (f // 128) + 128; in every block the first function's offset is the low end and the second function's the high end. pairs[A, 1] is 1; the list is symmetric, pairs[A, 1 + k] = pairs[A + k, 1 - k]; entries whose block A + k lies outside 0 to 31 are 0.
All inputs are finite; a program needn't handle non-finite values.
Results may differ from the reference program's by a relative error of at most 0.0003.
Values sent between devices are 32-bit elements; how exact they have to be, the bound alone decides.
A program may use at most 128 MiB of HBM per device.

```python
import math
import jax
import jax.numpy as jnp
from jax import lax

BLOCK_FUNCTIONS = 128
PATCH = 256
SPREAD = 128
SLOT_COUNT = 3
BSTEP = 192
SEG = 16384
NF = 4096
BLOCK_TOTAL = 32


def draw_offsets(key, part):
    rows_all = jnp.arange(NF, dtype=jnp.int32)
    within = rows_all % BLOCK_FUNCTIONS
    spread_draw = jax.random.randint(key, (NF,), 0, SPREAD + 1, dtype=jnp.int32)
    spread_draw = jnp.where(within == 0, 0, jnp.where(within == 1, SPREAD, spread_draw))
    return (BSTEP * (rows_all // BLOCK_FUNCTIONS) + spread_draw).astype(jnp.int32)


def draw_pairs(key, part):
    blocks_within_reach = (SLOT_COUNT - 1) // 2
    listed = (jax.random.randint(key, (BLOCK_TOTAL, blocks_within_reach), 0, 4, dtype=jnp.int32) > 0).astype(jnp.int32)
    blocks_all = jnp.arange(BLOCK_TOTAL, dtype=jnp.int32)
    columns = []
    for block_distance in range(-blocks_within_reach, blocks_within_reach + 1):
        if block_distance == 0:
            columns.append(jnp.ones((BLOCK_TOTAL,), jnp.int32))
        elif block_distance > 0:
            inside = blocks_all + block_distance < BLOCK_TOTAL
            columns.append(jnp.where(inside, listed[:, block_distance - 1], 0).astype(jnp.int32))
        else:
            inside = blocks_all + block_distance >= 0
            columns.append(jnp.where(inside, jnp.roll(listed[:, -block_distance - 1], -block_distance), 0).astype(jnp.int32))
    return jnp.stack(columns, axis=1)


def level_of(own_key, extent, cuts, low, top_value):
    loudness, own = 1.0, jax.random.fold_in(own_key, 6)
    for axis_at, parts in cuts:
        heights = jnp.exp(jax.random.uniform(jax.random.fold_in(own, axis_at), (parts,), jnp.float32, low / len(cuts), top_value / len(cuts)))
        loudness = loudness * jnp.repeat(heights, extent[axis_at] // parts).reshape([-1 if axis == axis_at else 1 for axis in range(len(extent))])
    return loudness


def centred(rng, dims, deviation, limit, shards=(), kind=jnp.bfloat16):
    values = jax.random.normal(rng, dims, jnp.float32) * deviation
    if len(shards) > 0:
        values = level_of(rng, dims, shards, -0.22, 0.18) * values
    return jnp.clip(values, min=-limit, max=limit).astype(kind)


def setup_inputs(seed: int = 0) -> dict:
    streams_of = jax.random.split(jax.random.key(seed), 5)
    orbitals = centred(streams_of[0], (2, NF, SEG), 0.25, 1.5, ((1, 32), (2, 8)), jnp.float32)
    offsets = draw_offsets(jax.random.fold_in(streams_of[4], 71), 0)
    pairs = draw_pairs(jax.random.fold_in(streams_of[4], 71), 0)
    kernel = centred(streams_of[3], (BLOCK_TOTAL, SLOT_COUNT, BLOCK_FUNCTIONS, BLOCK_FUNCTIONS), 0.1, 0.6, ((0, 32),), jnp.float32)
    return {"orbitals": orbitals, "offsets": offsets, "pairs": pairs, "kernel": kernel}


def position_row(segment, column_shift, window):
    blank = jnp.zeros((segment.shape[0], window), segment.dtype)
    return lax.dynamic_update_slice(blank, segment, (jnp.int32(0), column_shift))

def place_rows(segments, shifts, window):

    def inner(member_rows):
        return jax.vmap(lambda segment, column_shift: position_row(segment, column_shift, window))(member_rows, shifts)
    return jax.vmap(inner)(segments)

def pick_row(window_row, column_shift, patch):
    return lax.dynamic_slice(window_row, (jnp.int32(0), column_shift), (window_row.shape[0], patch))

def aligned(own_part, near_part, lag_cols):
    window = own_part.shape[-1]
    if lag_cols >= 0:
        return (own_part[..., lag_cols:], near_part[..., :window - lag_cols])
    return (own_part[..., :window + lag_cols], near_part[..., -lag_cols:])

def reference(orbitals, offsets, pairs, kernel):
    members, total_rows, seg_len = orbitals.shape
    planes = seg_len // PATCH
    window = PATCH + SPREAD
    block_count = total_rows // BLOCK_FUNCTIONS
    blocks_within_reach = (pairs.shape[1] - 1) // 2
    rows_all = jnp.arange(total_rows, dtype=jnp.int32)
    shifts = jnp.clip(offsets - BSTEP * (rows_all // BLOCK_FUNCTIONS), 0, SPREAD)
    volume = 1.0 / math.sqrt(SEG)

    def windows_of(block):
        start = (jnp.clip(block, 0, block_count - 1) * BLOCK_FUNCTIONS).astype(jnp.int32)
        block_rows = lax.dynamic_slice_in_dim(orbitals, start, BLOCK_FUNCTIONS, axis=1).reshape(members, BLOCK_FUNCTIONS, planes, PATCH)
        block_shift = lax.dynamic_slice_in_dim(shifts, start, BLOCK_FUNCTIONS)
        return (place_rows(block_rows, block_shift, window), block_shift)

    def one_block(block):
        own_windows, own_shift = windows_of(block)
        pair_row = lax.dynamic_index_in_dim(pairs, block, 0, keepdims=False).astype(jnp.float32)
        kernel_row = lax.dynamic_index_in_dim(kernel, block, 0, keepdims=False)
        accumulated = jnp.zeros((BLOCK_FUNCTIONS, planes, window), jnp.float32)
        for block_distance in range(-blocks_within_reach, blocks_within_reach + 1):
            slot_index = block_distance + blocks_within_reach
            nearby, unused_shift = windows_of(block + block_distance)
            lag_cols = block_distance * BSTEP
            own_part, near_part = aligned(own_windows[0], nearby[1], lag_cols)
            hamilton = volume * jnp.einsum('ixc,jxc->ij', own_part, near_part, precision=lax.Precision.HIGHEST)
            hamilton = hamilton * pair_row[slot_index]
            kernel_block = kernel_row[slot_index] * pair_row[slot_index]
            if lag_cols >= 0:
                target = slice(lag_cols, window)
                source = slice(0, window - lag_cols)
            else:
                target = slice(0, window + lag_cols)
                source = slice(-lag_cols, window)
            contribution = jnp.einsum('ij,jxc->ixc', kernel_block, nearby[1][..., source], precision=lax.Precision.HIGHEST)
            contribution = contribution - jnp.einsum('ij,jxc->ixc', hamilton, nearby[0][..., source], precision=lax.Precision.HIGHEST)
            accumulated = accumulated.at[..., target].add(contribution)
        picked = jax.vmap(lambda window_row, column_shift: pick_row(window_row, column_shift, PATCH))(accumulated, own_shift)
        return picked.reshape(BLOCK_FUNCTIONS, planes * PATCH)
    result = lax.map(one_block, jnp.arange(block_count, dtype=jnp.int32))
    return result.reshape(total_rows, seg_len)
```

```python
import functools
import math

import jax
import jax.numpy as jnp
from jax import lax
from jax.experimental import pallas as pl
from jax.experimental.pallas import tpu as pltpu
from jax.sharding import PartitionSpec as P

BLOCK = 128
PATCH = 256
SPREAD = 128
BSTEP = 192
SEG = 16384
QUARTERS = 4
PLANES_PER_CHUNK = 2
CHUNK_IN = PLANES_PER_CHUNK * PATCH
CHUNK = PLANES_PER_CHUNK * BSTEP
MESH = pl.DeviceIdType.MESH
LEFT, RIGHT = 0, 1
SIDE_SLOT = (0, 2)


def lane_gather(tile, index):
    return jnp.take_along_axis(tile, index, axis=1, mode="promise_in_bounds")


def split_rows(value):
    high = value.astype(jnp.bfloat16)
    low = (value - high.astype(jnp.float32)).astype(jnp.bfloat16)
    return high, low


def fold(square):
    return square[:BLOCK] + square[BLOCK:]


def place(planes, u, lane):
    idx_a = jnp.bitwise_and(lane - u, 127)
    idx_b = jnp.bitwise_and(lane - u + 64, 127)
    x0, x1, y0, y1 = (planes[:, i * 128 : (i + 1) * 128] for i in range(4))
    ax0, ax1, ay0, ay1 = (lane_gather(t, idx_a) for t in (x0, x1, y0, y1))
    bx0, bx1, by0, by1 = (lane_gather(t, idx_b) for t in (x0, x1, y0, y1))
    zero = jnp.zeros_like(x0)
    first = lane < 64
    at_u = lane < u
    over = lane < u + 64
    under = lane < u - 64
    left = (
        jnp.where(at_u, zero, ax0),
        jnp.where(at_u, zero, ay0),
        jnp.where(first, jnp.where(at_u, ax0, ax1), jnp.where(over, by0, by1)),
    )
    right = (
        jnp.where(under, bx0, jnp.where(over, bx1, zero)),
        jnp.where(under, by0, jnp.where(over, by1, zero)),
        jnp.where(
            first, jnp.where(under, bx1, zero), jnp.where(at_u, ay1, zero)
        ),
    )
    return left, right


def pick(left, right, u, lane):
    idx_a = jnp.bitwise_and(lane + u, 127)
    idx_b = jnp.bitwise_and(lane + u + 64, 127)
    l0, l1, l2 = (left[:, i * 128 : (i + 1) * 128] for i in range(3))
    r0, r1, r2 = (right[:, i * 128 : (i + 1) * 128] for i in range(3))
    column = lane + u
    outs = []
    for l_full, r_full, near, far in ((l0, r0, idx_a, idx_b), (l1, r1, idx_b, idx_a)):
        gl = lane_gather(l_full, idx_a)
        gm = lane_gather(l2, near)
        gr = lane_gather(r_full, idx_b)
        ge = lane_gather(r2, far)
        outs.append(jnp.where(column < 128, gl, jnp.where(column < 192, gm, gr)))
        outs.append(jnp.where(column < 64, gm, jnp.where(column < 192, gr, ge)))
    return outs


def body(
    n_orb, n_slab, orb_hbm, off_ref, pairs_ref, ker_ref, out_hbm,
    x_in, own, got, own_b, got_b, shift, hacc, hpart, hin, hsum, mats, total, outv,
    in_sem, send_sem, recv_sem, rs_send, rs_recv, ag_send, ag_recv, out_sem,
):
    me = lax.axis_index("orb")
    mine = lax.axis_index("slab")
    before = lax.rem(me + n_orb - 1, n_orb)
    after = lax.rem(me + 1, n_orb)
    rows = BLOCK // n_slab

    def load(m, q):
        return pltpu.make_async_copy(
            orb_hbm.at[m, :, pl.ds(pl.multiple_of(q * CHUNK_IN, CHUNK_IN), CHUNK_IN)],
            x_in.at[m, q], in_sem.at[m, q],
        )

    def send(m, side, q):
        return pltpu.make_async_remote_copy(
            src_ref=own.at[m, side, q], dst_ref=got.at[m, side, q],
            send_sem=send_sem.at[m, side, q], recv_sem=recv_sem.at[m, side, q],
            device_id=(before if side == LEFT else after, mine), device_id_type=MESH,
        )

    def store_out(q):
        return pltpu.make_async_copy(
            outv.at[q],
            out_hbm.at[:, pl.ds(pl.multiple_of(q * CHUNK_IN, CHUNK_IN), CHUNK_IN)],
            out_sem.at[q],
        )

    for m in (1, 0):
        for q in range(QUARTERS):
            load(m, q).start()

    barrier = pltpu.get_barrier_semaphore()
    pl.semaphore_signal(barrier, inc=1, device_id=(before, mine), device_id_type=MESH)
    pl.semaphore_signal(barrier, inc=1, device_id=(after, mine), device_id_type=MESH)
    for d in range(1, n_slab):
        peer = lax.rem(mine + d, n_slab)
        pl.semaphore_signal(barrier, inc=1, device_id=(me, peer), device_id_type=MESH)

    offset_row = off_ref[pl.ds(me, 1), :] - BSTEP * me
    shift[...] = jnp.transpose(jnp.broadcast_to(offset_row, (BLOCK, BLOCK)))
    lane = lax.broadcasted_iota(jnp.int32, (BLOCK, BLOCK), 1)
    pl.semaphore_wait(barrier, 2 + n_slab - 1)

    def place_chunk(m, q):
        left, right = place(x_in[m, q], shift[...], lane)
        for side, tiles in ((LEFT, left), (RIGHT, right)):
            for i, tile in enumerate(tiles):
                own[m, side, q, :, i * 128 : (i + 1) * 128] = tile

    def split_own(m, q):
        for side in (LEFT, RIGHT):
            high, low = split_rows(own[m, side, q])
            own_b[m, side, q, :BLOCK, :] = high
            own_b[m, side, q, BLOCK:, :] = low

    def first_step(q, carry):
        load(1, q).wait()
        place_chunk(1, q)
        send(1, LEFT, q).start()
        send(1, RIGHT, q).start()
        return carry

    lax.fori_loop(0, QUARTERS, first_step, 0)

    for k in range(3):
        weight = pairs_ref[0, k].astype(jnp.float32)
        high, low = split_rows(ker_ref[0, k] * weight)
        for j in range(2):
            mats[k, 1, :BLOCK, j * BLOCK : (j + 1) * BLOCK] = high
            mats[k, 1, BLOCK:, j * BLOCK : (j + 1) * BLOCK] = low
        hacc[k] = jnp.zeros((2 * BLOCK, 2 * BLOCK), jnp.float32)

    def across(a, b):
        return lax.dot_general(
            a, b, (((1,), (1,)), ((), ())), preferred_element_type=jnp.float32
        )

    def second_step(q, carry):
        load(0, q).wait()
        place_chunk(0, q)
        split_own(1, q)
        split_own(0, q)
        for side in (LEFT, RIGHT):
            hacc[1] += across(own_b[0, side, q], own_b[1, side, q])
        return carry

    lax.fori_loop(0, QUARTERS, second_step, 0)

    def split_got(m, side, q):
        high, low = split_rows(got[m, side, q])
        got_b[m, side, q, :BLOCK, :] = high
        got_b[m, side, q, BLOCK:, :] = low

    def third_step(q, carry):
        for side in (LEFT, RIGHT):
            send(1, side, q).wait_recv()
            send(0, side, q).start()
        for side in (LEFT, RIGHT):
            split_got(1, side, q)
            hacc[2 - 2 * side] += across(own_b[0, 1 - side, q], got_b[1, side, q])
        return carry

    lax.fori_loop(0, QUARTERS, third_step, 0)

    for k in range(3):
        square = fold(hacc[k])
        hpart[k] = square[:, :BLOCK] + square[:, BLOCK:]

    def spread(d):
        peer = lax.rem(mine + d, n_slab)
        return pltpu.make_async_remote_copy(
            src_ref=hpart.at[:, pl.ds(pl.multiple_of(peer * rows, rows), rows), :],
            dst_ref=hin.at[d],
            send_sem=rs_send.at[d], recv_sem=rs_recv.at[d],
            device_id=(me, peer), device_id_type=MESH,
        )

    def share(d):
        peer = lax.rem(mine + d, n_slab)
        here = pl.ds(pl.multiple_of(mine * rows, rows), rows)
        return pltpu.make_async_remote_copy(
            src_ref=hsum.at[:, here, :], dst_ref=hsum.at[:, here, :],
            send_sem=ag_send.at[d], recv_sem=ag_recv.at[d],
            device_id=(me, peer), device_id_type=MESH,
        )

    for d in range(1, n_slab):
        spread(d).start()

    def times(k, m, stack):
        return fold(jnp.dot(mats[k, m], stack, preferred_element_type=jnp.float32))

    def kernel_step(q, carry):
        for side in (LEFT, RIGHT):
            other = 1 - side
            total[side, q] = times(1, 1, own_b[1, side, q]) + times(
                2 * side, 1, got_b[1, other, q]
            )
        return carry

    lax.fori_loop(0, QUARTERS, kernel_step, 0)

    mine_rows = pl.ds(pl.multiple_of(mine * rows, rows), rows)
    piece = hpart[:, mine_rows, :]
    for d in range(1, n_slab):
        spread(d).wait_recv()
        piece += hin[d]
    hsum[:, mine_rows, :] = piece
    for d in range(1, n_slab):
        share(d).start()
    for d in range(1, n_slab):
        share(d).wait_recv()

    volume = 1.0 / math.sqrt(SEG)
    for k in range(3):
        weight = pairs_ref[0, k].astype(jnp.float32)
        high, low = split_rows(hsum[k] * (-volume * weight))
        for j in range(2):
            mats[k, 0, :BLOCK, j * BLOCK : (j + 1) * BLOCK] = high
            mats[k, 0, BLOCK:, j * BLOCK : (j + 1) * BLOCK] = low

    def own_step(q, carry):
        for side in (LEFT, RIGHT):
            total[side, q] += times(1, 0, own_b[0, side, q])
        return carry

    lax.fori_loop(0, QUARTERS, own_step, 0)

    def last_step(q, carry):
        sums = []
        for side in (LEFT, RIGHT):
            send(0, 1 - side, q).wait_recv()
            split_got(0, 1 - side, q)
            sums.append(total[side, q] + times(2 * side, 0, got_b[0, 1 - side, q]))
        for i, tile in enumerate(pick(sums[0], sums[1], shift[...], lane)):
            outv[q, :, i * 128 : (i + 1) * 128] = tile
        store_out(q).start()
        return carry

    lax.fori_loop(0, QUARTERS, last_step, 0)

    for d in range(1, n_slab):
        spread(d).wait_send()
        share(d).wait_send()
    for q in range(QUARTERS):
        for m in range(2):
            for side in (LEFT, RIGHT):
                send(m, side, q).wait_send()
        store_out(q).wait()


def per_device(n_orb, n_slab, orbitals, offsets, pairs, kernel):
    f32, b16 = jnp.float32, jnp.bfloat16
    dma = pltpu.SemaphoreType.DMA
    vmem = pl.BlockSpec(memory_space=pltpu.VMEM)
    return pl.pallas_call(
        functools.partial(body, n_orb, n_slab),
        out_shape=jax.ShapeDtypeStruct((BLOCK, QUARTERS * CHUNK_IN), f32),
        in_specs=[
            pl.BlockSpec(memory_space=pl.ANY), vmem,
            pl.BlockSpec(memory_space=pltpu.SMEM), vmem,
        ],
        out_specs=pl.BlockSpec(memory_space=pl.ANY),
        scratch_shapes=[
            pltpu.VMEM((2, QUARTERS, BLOCK, CHUNK_IN), f32),
            pltpu.VMEM((2, 2, QUARTERS, BLOCK, CHUNK), f32),
            pltpu.VMEM((2, 2, QUARTERS, BLOCK, CHUNK), f32),
            pltpu.VMEM((2, 2, QUARTERS, 2 * BLOCK, CHUNK), b16),
            pltpu.VMEM((2, 2, QUARTERS, 2 * BLOCK, CHUNK), b16),
            pltpu.VMEM((BLOCK, BLOCK), jnp.int32),
            pltpu.VMEM((3, 2 * BLOCK, 2 * BLOCK), f32),
            pltpu.VMEM((3, BLOCK, BLOCK), f32),
            pltpu.VMEM((n_slab, 3, BLOCK // n_slab, BLOCK), f32),
            pltpu.VMEM((3, BLOCK, BLOCK), f32),
            pltpu.VMEM((3, 2, 2 * BLOCK, 2 * BLOCK), b16),
            pltpu.VMEM((2, QUARTERS, BLOCK, CHUNK), f32),
            pltpu.VMEM((QUARTERS, BLOCK, CHUNK_IN), f32),
            dma((2, QUARTERS)), dma((2, 2, QUARTERS)), dma((2, 2, QUARTERS)),
            dma((n_slab,)), dma((n_slab,)), dma((n_slab,)), dma((n_slab,)),
            dma((QUARTERS,)),
        ],
        compiler_params=pltpu.CompilerParams(
            collective_id=0, has_side_effects=True, vmem_limit_bytes=40 * 2**20
        ),
        cost_estimate=pl.CostEstimate(
            flops=2400 * 10**6, bytes_accessed=4 * 2**20, transcendentals=0
        ),
    )(orbitals, offsets.reshape(n_orb, BLOCK), pairs, kernel)


def solution(mesh):
    n_orb, n_slab = mesh.shape["orb"], mesh.shape["slab"]
    placed = (P(None, "orb", "slab"), P(), P("orb", None), P("orb", None, None, None))
    return jax.shard_map(
        functools.partial(per_device, n_orb, n_slab), mesh=mesh, in_specs=placed,
        out_specs=P("orb", "slab"), check_vma=False,
    )
```

```python
import functools
import math

import jax
import jax.numpy as jnp
from jax import lax
from jax.experimental import pallas as pl
from jax.experimental.pallas import tpu as pltpu
from jax.sharding import PartitionSpec as P

BLOCK = 128
PATCH = 256
SPREAD = 128
BSTEP = 192
SEG = 16384
QUARTERS = 4
PLANES_PER_CHUNK = 2
CHUNK_IN = PLANES_PER_CHUNK * PATCH
CHUNK = PLANES_PER_CHUNK * BSTEP
MESH = pl.DeviceIdType.MESH
LEFT, RIGHT = 0, 1
SIDE_SLOT = (0, 2)


def lane_gather(tile, index):
    return jnp.take_along_axis(tile, index, axis=1, mode="promise_in_bounds")


def split_rows(value):
    high = value.astype(jnp.bfloat16)
    low = (value - high.astype(jnp.float32)).astype(jnp.bfloat16)
    return high, low


def fold(square):
    return square[:BLOCK] + square[BLOCK:]


def place(planes, u, lane):
    idx_a = jnp.bitwise_and(lane - u, 127)
    idx_b = jnp.bitwise_and(lane - u + 64, 127)
    x0, x1, y0, y1 = (planes[:, i * 128 : (i + 1) * 128] for i in range(4))
    ax0, ax1, ay0, ay1 = (lane_gather(t, idx_a) for t in (x0, x1, y0, y1))
    bx0, bx1, by0, by1 = (lane_gather(t, idx_b) for t in (x0, x1, y0, y1))
    zero = jnp.zeros_like(x0)
    first = lane < 64
    at_u = lane < u
    over = lane < u + 64
    under = lane < u - 64
    left = (
        jnp.where(at_u, zero, ax0),
        jnp.where(at_u, zero, ay0),
        jnp.where(first, jnp.where(at_u, ax0, ax1), jnp.where(over, by0, by1)),
    )
    right = (
        jnp.where(under, bx0, jnp.where(over, bx1, zero)),
        jnp.where(under, by0, jnp.where(over, by1, zero)),
        jnp.where(
            first, jnp.where(under, bx1, zero), jnp.where(at_u, ay1, zero)
        ),
    )
    return left, right


def pick(left, right, u, lane):
    idx_a = jnp.bitwise_and(lane + u, 127)
    idx_b = jnp.bitwise_and(lane + u + 64, 127)
    l0, l1, l2 = (left[:, i * 128 : (i + 1) * 128] for i in range(3))
    r0, r1, r2 = (right[:, i * 128 : (i + 1) * 128] for i in range(3))
    column = lane + u
    outs = []
    for l_full, r_full, near, far in ((l0, r0, idx_a, idx_b), (l1, r1, idx_b, idx_a)):
        gl = lane_gather(l_full, idx_a)
        gm = lane_gather(l2, near)
        gr = lane_gather(r_full, idx_b)
        ge = lane_gather(r2, far)
        outs.append(jnp.where(column < 128, gl, jnp.where(column < 192, gm, gr)))
        outs.append(jnp.where(column < 64, gm, jnp.where(column < 192, gr, ge)))
    return outs


def body(
    n_orb, n_slab, orb_hbm, off_hbm, pairs_hbm, ker_hbm, out_hbm,
    off_ref, pairs_ref, ker_ref, x_in, own, got, own_b, got_b, shift, hacc, hpart, hin, hsum, mats, total, outv,
    in_sem, send_sem, recv_sem, rs_send, rs_recv, ag_send, ag_recv, out_sem, small_sem,
):
    me = lax.axis_index("orb")
    mine = lax.axis_index("slab")
    has_before = me > 0
    has_after = me < n_orb - 1
    before = jnp.maximum(me - 1, 0)
    after = jnp.minimum(me + 1, n_orb - 1)
    rows = BLOCK // n_slab

    def load(m, q):
        return pltpu.make_async_copy(
            orb_hbm.at[m, :, pl.ds(pl.multiple_of(q * CHUNK_IN, CHUNK_IN), CHUNK_IN)],
            x_in.at[m, q], in_sem.at[m, q],
        )

    def send(m, side, q):
        return pltpu.make_async_remote_copy(
            src_ref=own.at[m, side, q], dst_ref=got.at[m, side, q],
            send_sem=send_sem.at[m, side, q], recv_sem=recv_sem.at[m, side, q],
            device_id=(before if side == LEFT else after, mine), device_id_type=MESH,
        )

    def store_out(q):
        return pltpu.make_async_copy(
            outv.at[q],
            out_hbm.at[:, pl.ds(pl.multiple_of(q * CHUNK_IN, CHUNK_IN), CHUNK_IN)],
            out_sem.at[q],
        )

    def if_goes(side, action):
        pl.when(has_before if side == LEFT else has_after)(action)

    def if_comes(side, action):
        pl.when(has_after if side == LEFT else has_before)(action)

    small = [
        pltpu.make_async_copy(src, dst, small_sem.at[i])
        for i, (src, dst) in enumerate(
            ((off_hbm, off_ref), (pairs_hbm, pairs_ref), (ker_hbm, ker_ref))
        )
    ]
    barrier = pltpu.get_barrier_semaphore()

    def greet(device):
        pl.semaphore_signal(barrier, inc=1, device_id=device, device_id_type=MESH)

    small[0].start()
    load(1, 0).start()
    if_goes(LEFT, lambda: greet((before, mine)))
    if_goes(RIGHT, lambda: greet((after, mine)))
    for d in range(1, n_slab):
        peer = lax.rem(mine + d, n_slab)
        greet((me, peer))
    for q in range(1, QUARTERS):
        load(1, q).start()
    for q in range(QUARTERS):
        load(0, q).start()
    small[1].start()
    small[2].start()

    small[0].wait()
    offset_row = off_ref[pl.ds(me, 1), :] - BSTEP * me
    shift[...] = jnp.transpose(jnp.broadcast_to(offset_row, (BLOCK, BLOCK)))
    lane = lax.broadcasted_iota(jnp.int32, (BLOCK, BLOCK), 1)

    def place_chunk(m, q):
        left, right = place(x_in[m, q], shift[...], lane)
        for side, tiles in ((LEFT, left), (RIGHT, right)):
            for i, tile in enumerate(tiles):
                own[m, side, q, :, i * 128 : (i + 1) * 128] = tile

    def split_own(m, q):
        for side in (LEFT, RIGHT):
            high, low = split_rows(own[m, side, q])
            own_b[m, side, q, :BLOCK, :] = high
            own_b[m, side, q, BLOCK:, :] = low

    def send_both(m, q):
        if_goes(LEFT, lambda: send(m, LEFT, q).start())
        if_goes(RIGHT, lambda: send(m, RIGHT, q).start())

    load(1, 0).wait()
    place_chunk(1, 0)
    pl.semaphore_wait(
        barrier,
        n_slab - 1 + has_before.astype(jnp.int32) + has_after.astype(jnp.int32),
    )
    send_both(1, 0)

    def first_step(q, carry):
        load(1, q).wait()
        place_chunk(1, q)
        send_both(1, q)
        return carry

    lax.fori_loop(1, QUARTERS, first_step, 0)

    for side in (LEFT, RIGHT):

        @pl.when(jnp.logical_not(has_after if side == LEFT else has_before))
        def _():
            def blank(q, carry):
                for m in range(2):
                    got[m, side, q] = jnp.zeros((BLOCK, CHUNK), jnp.float32)
                return carry

            lax.fori_loop(0, QUARTERS, blank, 0)

    small[1].wait()
    small[2].wait()

    def listed(k):
        return jnp.broadcast_to(
            pairs_ref[0:1, k : k + 1].astype(jnp.float32), (BLOCK, BLOCK)
        )

    for k in range(3):
        high, low = split_rows(ker_ref[0, k] * listed(k))
        for j in range(2):
            mats[k, 1, :BLOCK, j * BLOCK : (j + 1) * BLOCK] = high
            mats[k, 1, BLOCK:, j * BLOCK : (j + 1) * BLOCK] = low
        hacc[k] = jnp.zeros((2 * BLOCK, 2 * BLOCK), jnp.float32)

    def across(a, b):
        return lax.dot_general(
            a, b, (((1,), (1,)), ((), ())), preferred_element_type=jnp.float32
        )

    def second_step(q, carry):
        load(0, q).wait()
        place_chunk(0, q)
        split_own(1, q)
        split_own(0, q)
        for side in (LEFT, RIGHT):
            hacc[1] += across(own_b[0, side, q], own_b[1, side, q])
        return carry

    lax.fori_loop(0, QUARTERS, second_step, 0)

    def split_got(m, side, q):
        high, low = split_rows(got[m, side, q])
        got_b[m, side, q, :BLOCK, :] = high
        got_b[m, side, q, BLOCK:, :] = low

    def third_step(q, carry):
        for side in (LEFT, RIGHT):
            if_comes(side, lambda: send(1, side, q).wait_recv())
        send_both(0, q)
        for side in (LEFT, RIGHT):
            split_got(1, side, q)
            hacc[2 - 2 * side] += across(own_b[0, 1 - side, q], got_b[1, side, q])
        return carry

    lax.fori_loop(0, QUARTERS, third_step, 0)

    for k in range(3):
        square = fold(hacc[k])
        hpart[k] = square[:, :BLOCK] + square[:, BLOCK:]

    def spread(d):
        peer = lax.rem(mine + d, n_slab)
        return pltpu.make_async_remote_copy(
            src_ref=hpart.at[:, pl.ds(pl.multiple_of(peer * rows, rows), rows), :],
            dst_ref=hin.at[d],
            send_sem=rs_send.at[d], recv_sem=rs_recv.at[d],
            device_id=(me, peer), device_id_type=MESH,
        )

    def share(d):
        peer = lax.rem(mine + d, n_slab)
        here = pl.ds(pl.multiple_of(mine * rows, rows), rows)
        return pltpu.make_async_remote_copy(
            src_ref=hsum.at[:, here, :], dst_ref=hsum.at[:, here, :],
            send_sem=ag_send.at[d], recv_sem=ag_recv.at[d],
            device_id=(me, peer), device_id_type=MESH,
        )

    for d in range(1, n_slab):
        spread(d).start()

    def times(k, m, stack):
        return fold(jnp.dot(mats[k, m], stack, preferred_element_type=jnp.float32))

    def kernel_step(q, carry):
        for side in (LEFT, RIGHT):
            other = 1 - side
            total[side, q] = times(1, 1, own_b[1, side, q]) + times(
                2 * side, 1, got_b[1, other, q]
            )
        return carry

    lax.fori_loop(0, QUARTERS, kernel_step, 0)

    mine_rows = pl.ds(pl.multiple_of(mine * rows, rows), rows)
    piece = hpart[:, mine_rows, :]
    for d in range(1, n_slab):
        spread(d).wait_recv()
        piece += hin[d]
    hsum[:, mine_rows, :] = piece
    for d in range(1, n_slab):
        share(d).start()
    for d in range(1, n_slab):
        share(d).wait_recv()

    volume = 1.0 / math.sqrt(SEG)
    for k in range(3):
        high, low = split_rows(hsum[k] * (-volume * listed(k)))
        for j in range(2):
            mats[k, 0, :BLOCK, j * BLOCK : (j + 1) * BLOCK] = high
            mats[k, 0, BLOCK:, j * BLOCK : (j + 1) * BLOCK] = low

    def own_step(q, carry):
        for side in (LEFT, RIGHT):
            total[side, q] += times(1, 0, own_b[0, side, q])
        return carry

    lax.fori_loop(0, QUARTERS, own_step, 0)

    def last_step(q, carry):
        sums = []
        for side in (LEFT, RIGHT):
            if_comes(1 - side, lambda: send(0, 1 - side, q).wait_recv())
            split_got(0, 1 - side, q)
            sums.append(total[side, q] + times(2 * side, 0, got_b[0, 1 - side, q]))
        for i, tile in enumerate(pick(sums[0], sums[1], shift[...], lane)):
            outv[q, :, i * 128 : (i + 1) * 128] = tile
        store_out(q).start()
        return carry

    lax.fori_loop(0, QUARTERS, last_step, 0)

    for d in range(1, n_slab):
        spread(d).wait_send()
        share(d).wait_send()
    for q in range(QUARTERS):
        for m in range(2):
            for side in (LEFT, RIGHT):
                if_goes(side, lambda: send(m, side, q).wait_send())
        store_out(q).wait()


def per_device(n_orb, n_slab, orbitals, offsets, pairs, kernel):
    f32, b16 = jnp.float32, jnp.bfloat16
    dma = pltpu.SemaphoreType.DMA
    hbm = pl.BlockSpec(memory_space=pltpu.HBM)
    return pl.pallas_call(
        functools.partial(body, n_orb, n_slab),
        out_shape=jax.ShapeDtypeStruct((BLOCK, QUARTERS * CHUNK_IN), f32),
        in_specs=[hbm] * 4,
        out_specs=hbm,
        scratch_shapes=[
            pltpu.VMEM((n_orb, BLOCK), jnp.int32),
            pltpu.VMEM(pairs.shape, jnp.int32),
            pltpu.VMEM(kernel.shape, f32),
            pltpu.VMEM((2, QUARTERS, BLOCK, CHUNK_IN), f32),
            pltpu.VMEM((2, 2, QUARTERS, BLOCK, CHUNK), f32),
            pltpu.VMEM((2, 2, QUARTERS, BLOCK, CHUNK), f32),
            pltpu.VMEM((2, 2, QUARTERS, 2 * BLOCK, CHUNK), b16),
            pltpu.VMEM((2, 2, QUARTERS, 2 * BLOCK, CHUNK), b16),
            pltpu.VMEM((BLOCK, BLOCK), jnp.int32),
            pltpu.VMEM((3, 2 * BLOCK, 2 * BLOCK), f32),
            pltpu.VMEM((3, BLOCK, BLOCK), f32),
            pltpu.VMEM((n_slab, 3, BLOCK // n_slab, BLOCK), f32),
            pltpu.VMEM((3, BLOCK, BLOCK), f32),
            pltpu.VMEM((3, 2, 2 * BLOCK, 2 * BLOCK), b16),
            pltpu.VMEM((2, QUARTERS, BLOCK, CHUNK), f32),
            pltpu.VMEM((QUARTERS, BLOCK, CHUNK_IN), f32),
            dma((2, QUARTERS)), dma((2, 2, QUARTERS)), dma((2, 2, QUARTERS)),
            dma((n_slab,)), dma((n_slab,)), dma((n_slab,)), dma((n_slab,)),
            dma((QUARTERS,)), dma((3,)),
        ],
        compiler_params=pltpu.CompilerParams(
            collective_id=0, has_side_effects=True, vmem_limit_bytes=60 * 2**20
        ),
        cost_estimate=pl.CostEstimate(
            flops=2400 * 10**6, bytes_accessed=4 * 2**20, transcendentals=0
        ),
    )(orbitals, offsets.reshape(n_orb, BLOCK), pairs, kernel)


def solution(mesh):
    n_orb, n_slab = mesh.shape["orb"], mesh.shape["slab"]
    placed = (P(None, "orb", "slab"), P(), P("orb", None), P("orb", None, None, None))
    return jax.shard_map(
        functools.partial(per_device, n_orb, n_slab), mesh=mesh, in_specs=placed,
        out_specs=P("orb", "slab"), check_vma=False,
    )
```

```python
import functools
import math

import jax
import jax.numpy as jnp
from jax import lax
from jax.experimental import pallas as pl
from jax.experimental.pallas import tpu as pltpu
from jax.sharding import PartitionSpec as P

BLOCK = 128
PATCH = 256
SPREAD = 128
BSTEP = 192
SEG = 16384
QUARTERS = 4
PLANES_PER_CHUNK = 2
CHUNK_IN = PLANES_PER_CHUNK * PATCH
CHUNK = PLANES_PER_CHUNK * BSTEP
MESH = pl.DeviceIdType.MESH
LEFT, RIGHT = 0, 1


def lane_gather(tile, index):
    return jnp.take_along_axis(tile, index, axis=1, mode="promise_in_bounds")


def split_rows(value):
    high = value.astype(jnp.bfloat16)
    low = (value - high.astype(jnp.float32)).astype(jnp.bfloat16)
    return high, low


def fold(square):
    return square[:BLOCK] + square[BLOCK:]


def place(planes, u, lane):
    idx_a = jnp.bitwise_and(lane - u, 127)
    idx_b = jnp.bitwise_and(lane - u + 64, 127)
    x0, x1, y0, y1 = (planes[:, i * 128 : (i + 1) * 128] for i in range(4))
    ax0, ax1, ay0, ay1 = (lane_gather(t, idx_a) for t in (x0, x1, y0, y1))
    bx0, bx1, by0, by1 = (lane_gather(t, idx_b) for t in (x0, x1, y0, y1))
    zero = jnp.zeros_like(x0)
    first = lane < 64
    at_u = lane < u
    over = lane < u + 64
    under = lane < u - 64
    left = (
        jnp.where(at_u, zero, ax0),
        jnp.where(at_u, zero, ay0),
        jnp.where(first, jnp.where(at_u, ax0, ax1), jnp.where(over, by0, by1)),
    )
    right = (
        jnp.where(under, bx0, jnp.where(over, bx1, zero)),
        jnp.where(under, by0, jnp.where(over, by1, zero)),
        jnp.where(
            first, jnp.where(under, bx1, zero), jnp.where(at_u, ay1, zero)
        ),
    )
    return left, right


def pick(left, right, u, lane):
    idx_a = jnp.bitwise_and(lane + u, 127)
    idx_b = jnp.bitwise_and(lane + u + 64, 127)
    l0, l1, l2 = (left[:, i * 128 : (i + 1) * 128] for i in range(3))
    r0, r1, r2 = (right[:, i * 128 : (i + 1) * 128] for i in range(3))
    column = lane + u
    outs = []
    for l_full, r_full, near, far in ((l0, r0, idx_a, idx_b), (l1, r1, idx_b, idx_a)):
        gl = lane_gather(l_full, idx_a)
        gm = lane_gather(l2, near)
        gr = lane_gather(r_full, idx_b)
        ge = lane_gather(r2, far)
        outs.append(jnp.where(column < 128, gl, jnp.where(column < 192, gm, gr)))
        outs.append(jnp.where(column < 64, gm, jnp.where(column < 192, gr, ge)))
    return outs


def body(
    n_orb, n_slab, orb_hbm, off_hbm, pairs_hbm, ker_hbm, out_ref,
    off_ref, pairs_ref, ker_ref, x_in, own, got, own_b, got_b, shift, hacc, hpart, hin, hsum, mats, total,
    in_sem, send_sem, recv_sem, rs_send, rs_recv, ag_send, ag_recv, small_sem,
):
    me = lax.axis_index("orb")
    mine = lax.axis_index("slab")
    has_before = me > 0
    has_after = me < n_orb - 1
    before = jnp.maximum(me - 1, 0)
    after = jnp.minimum(me + 1, n_orb - 1)
    rows = BLOCK // n_slab

    def load(m, q):
        return pltpu.make_async_copy(
            orb_hbm.at[m, :, pl.ds(pl.multiple_of(q * CHUNK_IN, CHUNK_IN), CHUNK_IN)],
            x_in.at[m, q], in_sem.at[m, q],
        )

    def send(m, side, q):
        return pltpu.make_async_remote_copy(
            src_ref=own.at[m, side, q], dst_ref=got.at[m, side, q],
            send_sem=send_sem.at[m, side, q], recv_sem=recv_sem.at[m, side, q],
            device_id=(before if side == LEFT else after, mine), device_id_type=MESH,
        )

    def if_goes(side, action):
        pl.when(has_before if side == LEFT else has_after)(action)

    def if_comes(side, action):
        pl.when(has_after if side == LEFT else has_before)(action)

    small = [
        pltpu.make_async_copy(src, dst, small_sem.at[i])
        for i, (src, dst) in enumerate(
            ((off_hbm, off_ref), (pairs_hbm, pairs_ref), (ker_hbm, ker_ref))
        )
    ]
    barrier = pltpu.get_barrier_semaphore()

    def greet(device):
        pl.semaphore_signal(barrier, inc=1, device_id=device, device_id_type=MESH)

    small[0].start()
    load(1, 0).start()
    if_goes(LEFT, lambda: greet((before, mine)))
    if_goes(RIGHT, lambda: greet((after, mine)))
    for d in range(1, n_slab):
        peer = lax.rem(mine + d, n_slab)
        greet((me, peer))
    for q in range(1, QUARTERS):
        load(1, q).start()
    for q in range(QUARTERS):
        load(0, q).start()
    small[1].start()
    small[2].start()

    small[0].wait()
    offset_row = off_ref[pl.ds(me, 1), :] - BSTEP * me
    shift[...] = jnp.transpose(jnp.broadcast_to(offset_row, (BLOCK, BLOCK)))
    lane = lax.broadcasted_iota(jnp.int32, (BLOCK, BLOCK), 1)

    def place_chunk(m, q):
        left, right = place(x_in[m, q], shift[...], lane)
        for side, tiles in ((LEFT, left), (RIGHT, right)):
            for i, tile in enumerate(tiles):
                own[m, side, q, :, i * 128 : (i + 1) * 128] = tile

    def split_own(m, q):
        for side in (LEFT, RIGHT):
            high, low = split_rows(own[m, side, q])
            own_b[m, side, q, :BLOCK, :] = high
            own_b[m, side, q, BLOCK:, :] = low

    def send_both(m, q):
        if_goes(LEFT, lambda: send(m, LEFT, q).start())
        if_goes(RIGHT, lambda: send(m, RIGHT, q).start())

    load(1, 0).wait()
    place_chunk(1, 0)
    pl.semaphore_wait(
        barrier,
        n_slab - 1 + has_before.astype(jnp.int32) + has_after.astype(jnp.int32),
    )
    send_both(1, 0)

    def first_step(q, carry):
        load(1, q).wait()
        place_chunk(1, q)
        send_both(1, q)
        return carry

    lax.fori_loop(1, QUARTERS, first_step, 0)

    for side in (LEFT, RIGHT):

        @pl.when(jnp.logical_not(has_after if side == LEFT else has_before))
        def _():
            def blank(q, carry):
                for m in range(2):
                    got[m, side, q] = jnp.zeros((BLOCK, CHUNK), jnp.float32)
                return carry

            lax.fori_loop(0, QUARTERS, blank, 0)

    small[1].wait()
    small[2].wait()

    def listed(k):
        return jnp.broadcast_to(
            pairs_ref[0:1, k : k + 1].astype(jnp.float32), (BLOCK, BLOCK)
        )

    for k in range(3):
        high, low = split_rows(ker_ref[0, k] * listed(k))
        for j in range(2):
            mats[k, 1, :BLOCK, j * BLOCK : (j + 1) * BLOCK] = high
            mats[k, 1, BLOCK:, j * BLOCK : (j + 1) * BLOCK] = low
        hacc[k] = jnp.zeros((2 * BLOCK, 2 * BLOCK), jnp.float32)

    def across(a, b):
        return lax.dot_general(
            a, b, (((1,), (1,)), ((), ())), preferred_element_type=jnp.float32
        )

    def second_step(q, carry):
        load(0, q).wait()
        place_chunk(0, q)
        split_own(1, q)
        split_own(0, q)
        for side in (LEFT, RIGHT):
            hacc[1] += across(own_b[0, side, q], own_b[1, side, q])
        return carry

    lax.fori_loop(0, QUARTERS, second_step, 0)

    def split_got(m, side, q):
        high, low = split_rows(got[m, side, q])
        got_b[m, side, q, :BLOCK, :] = high
        got_b[m, side, q, BLOCK:, :] = low

    def third_step(q, carry):
        for side in (LEFT, RIGHT):
            if_comes(side, lambda: send(1, side, q).wait_recv())
        send_both(0, q)
        for side in (LEFT, RIGHT):
            split_got(1, side, q)
            hacc[2 - 2 * side] += across(own_b[0, 1 - side, q], got_b[1, side, q])
        return carry

    lax.fori_loop(0, QUARTERS, third_step, 0)

    for k in range(3):
        square = fold(hacc[k])
        hpart[k] = square[:, :BLOCK] + square[:, BLOCK:]

    def spread(d):
        peer = lax.rem(mine + d, n_slab)
        return pltpu.make_async_remote_copy(
            src_ref=hpart.at[:, pl.ds(pl.multiple_of(peer * rows, rows), rows), :],
            dst_ref=hin.at[d],
            send_sem=rs_send.at[d], recv_sem=rs_recv.at[d],
            device_id=(me, peer), device_id_type=MESH,
        )

    def share(d):
        peer = lax.rem(mine + d, n_slab)
        here = pl.ds(pl.multiple_of(mine * rows, rows), rows)
        return pltpu.make_async_remote_copy(
            src_ref=hsum.at[:, here, :], dst_ref=hsum.at[:, here, :],
            send_sem=ag_send.at[d], recv_sem=ag_recv.at[d],
            device_id=(me, peer), device_id_type=MESH,
        )

    for d in range(1, n_slab):
        spread(d).start()

    def times(k, m, stack):
        return fold(jnp.dot(mats[k, m], stack, preferred_element_type=jnp.float32))

    def kernel_step(q, carry):
        for side in (LEFT, RIGHT):
            other = 1 - side
            total[side, q] = times(1, 1, own_b[1, side, q]) + times(
                2 * side, 1, got_b[1, other, q]
            )
        return carry

    lax.fori_loop(0, QUARTERS, kernel_step, 0)

    mine_rows = pl.ds(pl.multiple_of(mine * rows, rows), rows)
    piece = hpart[:, mine_rows, :]
    for d in range(1, n_slab):
        spread(d).wait_recv()
        piece += hin[d]
    hsum[:, mine_rows, :] = piece
    for d in range(1, n_slab):
        share(d).start()
    for d in range(1, n_slab):
        share(d).wait_recv()

    volume = 1.0 / math.sqrt(SEG)
    for k in range(3):
        high, low = split_rows(hsum[k] * (-volume * listed(k)))
        for j in range(2):
            mats[k, 0, :BLOCK, j * BLOCK : (j + 1) * BLOCK] = high
            mats[k, 0, BLOCK:, j * BLOCK : (j + 1) * BLOCK] = low

    def own_step(q, carry):
        for side in (LEFT, RIGHT):
            total[side, q] += times(1, 0, own_b[0, side, q])
        return carry

    lax.fori_loop(0, QUARTERS, own_step, 0)

    def last_step(q, carry):
        sums = []
        for side in (LEFT, RIGHT):
            if_comes(1 - side, lambda: send(0, 1 - side, q).wait_recv())
            split_got(0, 1 - side, q)
            sums.append(total[side, q] + times(2 * side, 0, got_b[0, 1 - side, q]))
        for i, tile in enumerate(pick(sums[0], sums[1], shift[...], lane)):
            at = pl.multiple_of(q * CHUNK_IN + i * 128, 128)
            out_ref[:, pl.ds(at, 128)] = tile
        return carry

    lax.fori_loop(0, QUARTERS, last_step, 0)

    for d in range(1, n_slab):
        spread(d).wait_send()
        share(d).wait_send()
    for q in range(QUARTERS):
        for m in range(2):
            for side in (LEFT, RIGHT):
                if_goes(side, lambda: send(m, side, q).wait_send())


def per_device(n_orb, n_slab, orbitals, offsets, pairs, kernel):
    f32, b16 = jnp.float32, jnp.bfloat16
    dma = pltpu.SemaphoreType.DMA
    hbm = pl.BlockSpec(memory_space=pltpu.HBM)
    operands = [
        pltpu.with_memory_space_constraint(x, pltpu.HBM)
        for x in (orbitals, offsets.reshape(n_orb, BLOCK), pairs, kernel)
    ]
    return pl.pallas_call(
        functools.partial(body, n_orb, n_slab),
        out_shape=pltpu.VMEM((BLOCK, QUARTERS * CHUNK_IN), f32),
        in_specs=[hbm] * 4,
        out_specs=pl.BlockSpec(memory_space=pltpu.VMEM),
        scratch_shapes=[
            pltpu.VMEM((n_orb, BLOCK), jnp.int32),
            pltpu.VMEM(pairs.shape, jnp.int32),
            pltpu.VMEM(kernel.shape, f32),
            pltpu.VMEM((2, QUARTERS, BLOCK, CHUNK_IN), f32),
            pltpu.VMEM((2, 2, QUARTERS, BLOCK, CHUNK), f32),
            pltpu.VMEM((2, 2, QUARTERS, BLOCK, CHUNK), f32),
            pltpu.VMEM((2, 2, QUARTERS, 2 * BLOCK, CHUNK), b16),
            pltpu.VMEM((2, 2, QUARTERS, 2 * BLOCK, CHUNK), b16),
            pltpu.VMEM((BLOCK, BLOCK), jnp.int32),
            pltpu.VMEM((3, 2 * BLOCK, 2 * BLOCK), f32),
            pltpu.VMEM((3, BLOCK, BLOCK), f32),
            pltpu.VMEM((n_slab, 3, BLOCK // n_slab, BLOCK), f32),
            pltpu.VMEM((3, BLOCK, BLOCK), f32),
            pltpu.VMEM((3, 2, 2 * BLOCK, 2 * BLOCK), b16),
            pltpu.VMEM((2, QUARTERS, BLOCK, CHUNK), f32),
            dma((2, QUARTERS)), dma((2, 2, QUARTERS)), dma((2, 2, QUARTERS)),
            dma((n_slab,)), dma((n_slab,)), dma((n_slab,)), dma((n_slab,)),
            dma((3,)),
        ],
        compiler_params=pltpu.CompilerParams(
            collective_id=0, has_side_effects=True, vmem_limit_bytes=40 * 2**20
        ),
        cost_estimate=pl.CostEstimate(
            flops=2400 * 10**6, bytes_accessed=4 * 2**20, transcendentals=0
        ),
    )(*operands)


def solution(mesh):
    n_orb, n_slab = mesh.shape["orb"], mesh.shape["slab"]
    placed = (P(None, "orb", "slab"), P(), P("orb", None), P("orb", None, None, None))
    return jax.shard_map(
        functools.partial(per_device, n_orb, n_slab), mesh=mesh, in_specs=placed,
        out_specs=P("orb", "slab"), check_vma=False,
    )
```

```python
import functools
import math

import jax
import jax.numpy as jnp
from jax import lax
from jax.experimental import pallas as pl
from jax.experimental.pallas import tpu as pltpu
from jax.sharding import PartitionSpec as P

BLOCK = 128
PATCH = 256
SPREAD = 128
BSTEP = 192
SEG = 16384
QUARTERS = 4
PLANES_PER_CHUNK = 2
CHUNK_IN = PLANES_PER_CHUNK * PATCH
CHUNK = PLANES_PER_CHUNK * BSTEP
MESH = pl.DeviceIdType.MESH
LEFT, RIGHT = 0, 1
ROW = 8
VIA = QUARTERS - 1


def lane_gather(tile, index):
    return jnp.take_along_axis(tile, index, axis=1, mode="promise_in_bounds")


def split_rows(value):
    high = value.astype(jnp.bfloat16)
    low = (value - high.astype(jnp.float32)).astype(jnp.bfloat16)
    return high, low


def fold(square):
    return square[:BLOCK] + square[BLOCK:]


def place(planes, u, lane):
    idx_a = jnp.bitwise_and(lane - u, 127)
    idx_b = jnp.bitwise_and(lane - u + 64, 127)
    x0, x1, y0, y1 = (planes[:, i * 128 : (i + 1) * 128] for i in range(4))
    ax0, ax1, ay0, ay1 = (lane_gather(t, idx_a) for t in (x0, x1, y0, y1))
    bx0, bx1, by0, by1 = (lane_gather(t, idx_b) for t in (x0, x1, y0, y1))
    zero = jnp.zeros_like(x0)
    first = lane < 64
    at_u = lane < u
    over = lane < u + 64
    under = lane < u - 64
    left = (
        jnp.where(at_u, zero, ax0),
        jnp.where(at_u, zero, ay0),
        jnp.where(first, jnp.where(at_u, ax0, ax1), jnp.where(over, by0, by1)),
    )
    right = (
        jnp.where(under, bx0, jnp.where(over, bx1, zero)),
        jnp.where(under, by0, jnp.where(over, by1, zero)),
        jnp.where(
            first, jnp.where(under, bx1, zero), jnp.where(at_u, ay1, zero)
        ),
    )
    return left, right


def pick(left, right, u, lane):
    idx_a = jnp.bitwise_and(lane + u, 127)
    idx_b = jnp.bitwise_and(lane + u + 64, 127)
    l0, l1, l2 = (left[:, i * 128 : (i + 1) * 128] for i in range(3))
    r0, r1, r2 = (right[:, i * 128 : (i + 1) * 128] for i in range(3))
    column = lane + u
    outs = []
    for l_full, r_full, near, far in ((l0, r0, idx_a, idx_b), (l1, r1, idx_b, idx_a)):
        gl = lane_gather(l_full, idx_a)
        gm = lane_gather(l2, near)
        gr = lane_gather(r_full, idx_b)
        ge = lane_gather(r2, far)
        outs.append(jnp.where(column < 128, gl, jnp.where(column < 192, gm, gr)))
        outs.append(jnp.where(column < 64, gm, jnp.where(column < 192, gr, ge)))
    return outs


def body(
    n_orb, n_slab, orb_hbm, off_hbm, pairs_hbm, ker_hbm, out_ref,
    off_ref, pairs_ref, ker_ref, x_in, own, got, own_b, got_b, shift, hacc, hpart, hin, hsum, mats, total,
    in_sem, send_sem, recv_sem, rs_send, rs_recv, ag_send, ag_recv, small_sem,
    held, held_sem, onward_sem, ready_sem,
):
    me = lax.axis_index("orb")
    mine = lax.axis_index("slab")
    has_before = me > 0
    has_after = me < n_orb - 1
    before = jnp.maximum(me - 1, 0)
    after = jnp.minimum(me + 1, n_orb - 1)
    rows = BLOCK // n_slab

    flows = n_orb // ROW - 1
    last = n_orb - 1
    flow_end = lax.rem(me, ROW) == ROW - 1
    is_source = jnp.logical_and(flow_end, me < last)
    is_relay = me == last
    is_target = jnp.logical_and(lax.rem(me, ROW) == 0, me > 0)
    flow = me // ROW
    far = 1 if flows >= 3 else -1
    stop = (far + 1) * ROW + ROW - 1 if flows >= 3 else last
    is_stop = jnp.logical_and(me == stop, stop < last)
    via = jnp.where(flow == far, stop, last)

    def detour():
        return pltpu.make_async_remote_copy(
            src_ref=own.at[0, RIGHT, VIA], dst_ref=held.at[flow],
            send_sem=send_sem.at[0, RIGHT, VIA], recv_sem=held_sem.at[flow],
            device_id=(via, mine), device_id_type=MESH,
        )

    def onward(i):
        return pltpu.make_async_remote_copy(
            src_ref=held.at[i], dst_ref=got.at[0, RIGHT, VIA],
            send_sem=onward_sem.at[i], recv_sem=recv_sem.at[0, RIGHT, VIA],
            device_id=((i + 1) * ROW, mine), device_id_type=MESH,
        )

    def second_hop():
        return pltpu.make_async_remote_copy(
            src_ref=held.at[far], dst_ref=held.at[far],
            send_sem=onward_sem.at[far], recv_sem=held_sem.at[far],
            device_id=(last, mine), device_id_type=MESH,
        )

    def arrived(i):
        return pltpu.make_async_remote_copy(
            src_ref=held.at[i], dst_ref=held.at[i],
            send_sem=onward_sem.at[i], recv_sem=held_sem.at[i],
            device_id=(before, mine), device_id_type=MESH,
        )

    def load(m, q):
        return pltpu.make_async_copy(
            orb_hbm.at[m, :, pl.ds(pl.multiple_of(q * CHUNK_IN, CHUNK_IN), CHUNK_IN)],
            x_in.at[m, q], in_sem.at[m, q],
        )

    def send(m, side, q):
        return pltpu.make_async_remote_copy(
            src_ref=own.at[m, side, q], dst_ref=got.at[m, side, q],
            send_sem=send_sem.at[m, side, q], recv_sem=recv_sem.at[m, side, q],
            device_id=(before if side == LEFT else after, mine), device_id_type=MESH,
        )

    def if_goes(side, action):
        pl.when(has_before if side == LEFT else has_after)(action)

    def if_comes(side, action):
        pl.when(has_after if side == LEFT else has_before)(action)

    small = [
        pltpu.make_async_copy(src, dst, small_sem.at[i])
        for i, (src, dst) in enumerate(
            ((off_hbm, off_ref), (pairs_hbm, pairs_ref), (ker_hbm, ker_ref))
        )
    ]
    barrier = pltpu.get_barrier_semaphore()

    def greet(device):
        pl.semaphore_signal(barrier, inc=1, device_id=device, device_id_type=MESH)

    small[0].start()
    load(1, 0).start()
    if_goes(LEFT, lambda: greet((before, mine)))
    if_goes(RIGHT, lambda: greet((after, mine)))
    pl.when(is_source)(lambda: greet((via, mine)))
    pl.when(is_target)(lambda: greet((last, mine)))
    for d in range(1, n_slab):
        peer = lax.rem(mine + d, n_slab)
        greet((me, peer))
    for q in range(1, QUARTERS):
        load(1, q).start()
    for q in range(QUARTERS):
        load(0, q).start()
    small[1].start()
    small[2].start()

    small[0].wait()
    offset_row = off_ref[pl.ds(me, 1), :] - BSTEP * me
    shift[...] = jnp.transpose(jnp.broadcast_to(offset_row, (BLOCK, BLOCK)))
    lane = lax.broadcasted_iota(jnp.int32, (BLOCK, BLOCK), 1)

    def place_chunk(m, q):
        left, right = place(x_in[m, q], shift[...], lane)
        for side, tiles in ((LEFT, left), (RIGHT, right)):
            for i, tile in enumerate(tiles):
                own[m, side, q, :, i * 128 : (i + 1) * 128] = tile

    def split_own(m, q):
        for side in (LEFT, RIGHT):
            high, low = split_rows(own[m, side, q])
            own_b[m, side, q, :BLOCK, :] = high
            own_b[m, side, q, BLOCK:, :] = low

    def send_both(m, q):
        if_goes(LEFT, lambda: send(m, LEFT, q).start())
        if_goes(RIGHT, lambda: send(m, RIGHT, q).start())

    load(1, 0).wait()
    place_chunk(1, 0)
    pl.semaphore_wait(
        barrier,
        n_slab - 1 + has_before.astype(jnp.int32) + has_after.astype(jnp.int32)
        + (2 * flows - (far > 0)) * is_relay.astype(jnp.int32)
        + is_stop.astype(jnp.int32),
    )

    def ready(i):
        pl.semaphore_signal(
            ready_sem, inc=1, device_id=(i * ROW + ROW - 1, mine), device_id_type=MESH
        )


    @pl.when(is_relay)
    def _():
        for i in range(flows):
            if i != far:
                ready(i)

    if far > 0:
        pl.when(is_stop)(lambda: ready(far))

    send_both(1, 0)

    def first_step(q, carry):
        load(1, q).wait()
        place_chunk(1, q)
        send_both(1, q)
        return carry

    lax.fori_loop(1, QUARTERS, first_step, 0)

    for side in (LEFT, RIGHT):

        @pl.when(jnp.logical_not(has_after if side == LEFT else has_before))
        def _():
            def blank(q, carry):
                for m in range(2):
                    got[m, side, q] = jnp.zeros((BLOCK, CHUNK), jnp.float32)
                return carry

            lax.fori_loop(0, QUARTERS, blank, 0)

    small[1].wait()
    small[2].wait()

    def listed(k):
        return jnp.broadcast_to(
            pairs_ref[0:1, k : k + 1].astype(jnp.float32), (BLOCK, BLOCK)
        )

    for k in range(3):
        high, low = split_rows(ker_ref[0, k] * listed(k))
        for j in range(2):
            mats[k, 1, :BLOCK, j * BLOCK : (j + 1) * BLOCK] = high
            mats[k, 1, BLOCK:, j * BLOCK : (j + 1) * BLOCK] = low
        hacc[k] = jnp.zeros((2 * BLOCK, 2 * BLOCK), jnp.float32)

    def across(a, b):
        return lax.dot_general(
            a, b, (((1,), (1,)), ((), ())), preferred_element_type=jnp.float32
        )

    def second_step(q, carry):
        load(0, q).wait()
        place_chunk(0, q)
        split_own(1, q)
        split_own(0, q)
        for side in (LEFT, RIGHT):
            hacc[1] += across(own_b[0, side, q], own_b[1, side, q])
        return carry

    lax.fori_loop(0, QUARTERS, second_step, 0)

    @pl.when(is_source)
    def _():
        pl.semaphore_wait(ready_sem, 1)
        detour().start()

    def split_got(m, side, q):
        high, low = split_rows(got[m, side, q])
        got_b[m, side, q, :BLOCK, :] = high
        got_b[m, side, q, BLOCK:, :] = low

    def third_step(q, carry):
        for side in (LEFT, RIGHT):
            if_comes(side, lambda: send(1, side, q).wait_recv())
        if_goes(LEFT, lambda: send(0, LEFT, q).start())
        straight = jnp.logical_not(jnp.logical_and(is_source, q == VIA))
        pl.when(jnp.logical_and(has_after, straight))(
            lambda: send(0, RIGHT, q).start()
        )

        @pl.when(jnp.logical_and(is_relay, q == VIA - 1))
        def _():
            for i in range(flows):
                if i != far:
                    arrived(i).wait_recv()
                    onward(i).start()

        if far > 0:

            @pl.when(jnp.logical_and(is_stop, q == VIA - 2))
            def _():
                arrived(far).wait_recv()
                second_hop().start()

            @pl.when(jnp.logical_and(is_relay, q == VIA))
            def _():
                arrived(far).wait_recv()
                onward(far).start()

        for side in (LEFT, RIGHT):
            split_got(1, side, q)
            hacc[2 - 2 * side] += across(own_b[0, 1 - side, q], got_b[1, side, q])
        return carry

    lax.fori_loop(0, QUARTERS, third_step, 0)

    for k in range(3):
        square = fold(hacc[k])
        hpart[k] = square[:, :BLOCK] + square[:, BLOCK:]

    def spread(d):
        peer = lax.rem(mine + d, n_slab)
        return pltpu.make_async_remote_copy(
            src_ref=hpart.at[:, pl.ds(pl.multiple_of(peer * rows, rows), rows), :],
            dst_ref=hin.at[d],
            send_sem=rs_send.at[d], recv_sem=rs_recv.at[d],
            device_id=(me, peer), device_id_type=MESH,
        )

    def share(d):
        peer = lax.rem(mine + d, n_slab)
        here = pl.ds(pl.multiple_of(mine * rows, rows), rows)
        return pltpu.make_async_remote_copy(
            src_ref=hsum.at[:, here, :], dst_ref=hsum.at[:, here, :],
            send_sem=ag_send.at[d], recv_sem=ag_recv.at[d],
            device_id=(me, peer), device_id_type=MESH,
        )

    for d in range(1, n_slab):
        spread(d).start()

    def times(k, m, stack):
        return fold(jnp.dot(mats[k, m], stack, preferred_element_type=jnp.float32))

    def kernel_step(q, carry):
        for side in (LEFT, RIGHT):
            other = 1 - side
            total[side, q] = times(1, 1, own_b[1, side, q]) + times(
                2 * side, 1, got_b[1, other, q]
            )
        return carry

    lax.fori_loop(0, QUARTERS, kernel_step, 0)

    mine_rows = pl.ds(pl.multiple_of(mine * rows, rows), rows)
    piece = hpart[:, mine_rows, :]
    for d in range(1, n_slab):
        spread(d).wait_recv()
        piece += hin[d]
    hsum[:, mine_rows, :] = piece
    for d in range(1, n_slab):
        share(d).start()
    for d in range(1, n_slab):
        share(d).wait_recv()

    volume = 1.0 / math.sqrt(SEG)
    for k in range(3):
        high, low = split_rows(hsum[k] * (-volume * listed(k)))
        for j in range(2):
            mats[k, 0, :BLOCK, j * BLOCK : (j + 1) * BLOCK] = high
            mats[k, 0, BLOCK:, j * BLOCK : (j + 1) * BLOCK] = low

    def own_step(q, carry):
        for side in (LEFT, RIGHT):
            total[side, q] += times(1, 0, own_b[0, side, q])
        return carry

    lax.fori_loop(0, QUARTERS, own_step, 0)

    def last_step(q, carry):
        sums = []
        for side in (LEFT, RIGHT):
            if_comes(1 - side, lambda: send(0, 1 - side, q).wait_recv())
            split_got(0, 1 - side, q)
            sums.append(total[side, q] + times(2 * side, 0, got_b[0, 1 - side, q]))
        for i, tile in enumerate(pick(sums[0], sums[1], shift[...], lane)):
            at = pl.multiple_of(q * CHUNK_IN + i * 128, 128)
            out_ref[:, pl.ds(at, 128)] = tile
        return carry

    lax.fori_loop(0, QUARTERS, last_step, 0)

    @pl.when(is_relay)
    def _():
        for i in range(flows):
            onward(i).wait_send()

    if far > 0:
        pl.when(is_stop)(lambda: second_hop().wait_send())

    for d in range(1, n_slab):
        spread(d).wait_send()
        share(d).wait_send()
    for q in range(QUARTERS):
        for m in range(2):
            for side in (LEFT, RIGHT):
                if_goes(side, lambda: send(m, side, q).wait_send())


def per_device(n_orb, n_slab, orbitals, offsets, pairs, kernel):
    f32, b16 = jnp.float32, jnp.bfloat16
    dma = pltpu.SemaphoreType.DMA
    hbm = pl.BlockSpec(memory_space=pltpu.HBM)
    operands = [
        pltpu.with_memory_space_constraint(x, pltpu.HBM)
        for x in (orbitals, offsets.reshape(n_orb, BLOCK), pairs, kernel)
    ]
    return pl.pallas_call(
        functools.partial(body, n_orb, n_slab),
        out_shape=pltpu.VMEM((BLOCK, QUARTERS * CHUNK_IN), f32),
        in_specs=[hbm] * 4,
        out_specs=pl.BlockSpec(memory_space=pltpu.VMEM),
        scratch_shapes=[
            pltpu.VMEM((n_orb, BLOCK), jnp.int32),
            pltpu.VMEM(pairs.shape, jnp.int32),
            pltpu.VMEM(kernel.shape, f32),
            pltpu.VMEM((2, QUARTERS, BLOCK, CHUNK_IN), f32),
            pltpu.VMEM((2, 2, QUARTERS, BLOCK, CHUNK), f32),
            pltpu.VMEM((2, 2, QUARTERS, BLOCK, CHUNK), f32),
            pltpu.VMEM((2, 2, QUARTERS, 2 * BLOCK, CHUNK), b16),
            pltpu.VMEM((2, 2, QUARTERS, 2 * BLOCK, CHUNK), b16),
            pltpu.VMEM((BLOCK, BLOCK), jnp.int32),
            pltpu.VMEM((3, 2 * BLOCK, 2 * BLOCK), f32),
            pltpu.VMEM((3, BLOCK, BLOCK), f32),
            pltpu.VMEM((n_slab, 3, BLOCK // n_slab, BLOCK), f32),
            pltpu.VMEM((3, BLOCK, BLOCK), f32),
            pltpu.VMEM((3, 2, 2 * BLOCK, 2 * BLOCK), b16),
            pltpu.VMEM((2, QUARTERS, BLOCK, CHUNK), f32),
            dma((2, QUARTERS)), dma((2, 2, QUARTERS)), dma((2, 2, QUARTERS)),
            dma((n_slab,)), dma((n_slab,)), dma((n_slab,)), dma((n_slab,)),
            dma((3,)),
            pltpu.VMEM((n_orb // ROW - 1, BLOCK, CHUNK), f32),
            dma((n_orb // ROW - 1,)), dma((n_orb // ROW - 1,)),
            pltpu.SemaphoreType.REGULAR,
        ],
        compiler_params=pltpu.CompilerParams(
            collective_id=0, has_side_effects=True, vmem_limit_bytes=40 * 2**20
        ),
        cost_estimate=pl.CostEstimate(
            flops=2400 * 10**6, bytes_accessed=4 * 2**20, transcendentals=0
        ),
    )(*operands)


def solution(mesh):
    n_orb, n_slab = mesh.shape["orb"], mesh.shape["slab"]
    placed = (P(None, "orb", "slab"), P(), P("orb", None), P("orb", None, None, None))
    return jax.shard_map(
        functools.partial(per_device, n_orb, n_slab), mesh=mesh, in_specs=placed,
        out_specs=P("orb", "slab"), check_vma=False,
    )
```

```python
import functools
import math

import jax
import jax.numpy as jnp
from jax import lax
from jax.experimental import pallas as pl
from jax.experimental.pallas import tpu as pltpu
from jax.sharding import PartitionSpec as P

BLOCK = 128
PATCH = 256
SPREAD = 128
BSTEP = 192
SEG = 16384
QUARTERS = 4
PLANES = 2
CHUNK_IN = PLANES * PATCH
TILE = 64
TILES = BSTEP // TILE
CHUNK = PLANES * BSTEP
MOST_ROWS = 88
MESH = pl.DeviceIdType.MESH
LEFT, RIGHT = 0, 1
ROW = 8
VIA = QUARTERS - 1


def lane_gather(tile, index):
    return jnp.take_along_axis(tile, index, axis=1, mode="promise_in_bounds")


def split_rows(value):
    high = value.astype(jnp.bfloat16)
    low = (value - high.astype(jnp.float32)).astype(jnp.bfloat16)
    return high, low


def fold(square):
    return square[:BLOCK] + square[BLOCK:]


def place(planes, u, lane):
    merged = []
    for v in range(2):
        vregs = [planes[:, (2 * x + v) * 128 : (2 * x + v + 1) * 128] for x in range(PLANES)]
        row = []
        for s in range(PLANES):
            turned = [
                lane_gather(vregs[x], jnp.bitwise_and(lane + TILE * (s - x) - u, 127))
                for x in range(PLANES)
            ]
            row.append(jnp.where(lane < TILE, turned[0], turned[1]))
        merged.append(row)
    zero = jnp.zeros_like(merged[0][0])
    within = jnp.bitwise_and(lane, TILE - 1) - u
    left, right = [], []
    for t in range(TILES):
        at = within + TILE * t
        near, far = merged[0][t % 2], merged[1][t % 2]
        left.append(jnp.where(at < 0, zero, jnp.where(at < 128, near, far)))
        at = within + TILE * t + BSTEP
        near, far = merged[0][(t + 1) % 2], merged[1][(t + 1) % 2]
        right.append(jnp.where(at < 128, near, jnp.where(at < 256, far, zero)))
    return left, right


def pick(tiles, u, lane):
    column = lane + u
    outs = []
    for x in range(PLANES):
        index = jnp.bitwise_and(column, TILE - 1) + TILE * x
        turned = [lane_gather(tile, index) for tile in tiles]
        for first in (0, 2):
            value = turned[first + 3]
            for t in range(2, -1, -1):
                value = jnp.where(column < TILE * (t + 1), turned[first + t], value)
            outs.append(value)
    return outs


def pieces(side, most):
    if most == BLOCK:
        return ((0, BLOCK, 0, CHUNK),)
    if side == LEFT:
        return ((0, BLOCK, 128, CHUNK), (0, most, 0, 128))
    return ((0, BLOCK, 0, CHUNK - 128), (BLOCK - most, BLOCK, CHUNK - 128, CHUNK))


def body(
    n_orb, n_slab, most, orb_hbm, off_hbm, pairs_hbm, ker_hbm, out_ref, over_ref,
    off_ref, pairs_ref, ker_ref, x_in, own, got, own_b, got_b, shift, sorted_shift, sorter, hacc, hpart, hin, hsum, mats, total,
    in_sem, send_sem, recv_sem, rs_send, rs_recv, ag_send, ag_recv, small_sem,
    held, held_sem, onward_sem, ready_sem,
):
    me = lax.axis_index("orb")
    mine = lax.axis_index("slab")
    has_before = me > 0
    has_after = me < n_orb - 1
    before = jnp.maximum(me - 1, 0)
    after = jnp.minimum(me + 1, n_orb - 1)
    rows = BLOCK // n_slab

    flows = n_orb // ROW - 1
    last = n_orb - 1
    flow_end = lax.rem(me, ROW) == ROW - 1
    is_source = jnp.logical_and(flow_end, me < last)
    is_relay = me == last
    is_target = jnp.logical_and(lax.rem(me, ROW) == 0, me > 0)
    flow = me // ROW
    far = 1 if flows >= 3 else -1
    stop = (far + 1) * ROW + ROW - 1 if flows >= 3 else last
    is_stop = jnp.logical_and(me == stop, stop < last)
    via = jnp.where(flow == far, stop, last)

    def detour():
        return pltpu.make_async_remote_copy(
            src_ref=own.at[0, RIGHT, VIA], dst_ref=held.at[flow],
            send_sem=send_sem.at[0, RIGHT, VIA, 0], recv_sem=held_sem.at[flow],
            device_id=(via, mine), device_id_type=MESH,
        )

    def onward(i):
        return pltpu.make_async_remote_copy(
            src_ref=held.at[i], dst_ref=got.at[0, RIGHT, VIA],
            send_sem=onward_sem.at[i], recv_sem=recv_sem.at[0, RIGHT, VIA, 0],
            device_id=((i + 1) * ROW, mine), device_id_type=MESH,
        )

    def second_hop():
        return pltpu.make_async_remote_copy(
            src_ref=held.at[far], dst_ref=held.at[far],
            send_sem=onward_sem.at[far], recv_sem=held_sem.at[far],
            device_id=(last, mine), device_id_type=MESH,
        )

    def arrived(i):
        return pltpu.make_async_remote_copy(
            src_ref=held.at[i], dst_ref=held.at[i],
            send_sem=onward_sem.at[i], recv_sem=held_sem.at[i],
            device_id=(before, mine), device_id_type=MESH,
        )

    def load(m, q):
        return pltpu.make_async_copy(
            orb_hbm.at[m, :, pl.ds(pl.multiple_of(q * CHUNK_IN, CHUNK_IN), CHUNK_IN)],
            x_in.at[m, q], in_sem.at[m, q],
        )

    def send(m, side, q):
        copies = []
        for i, (top, bottom, first, end) in enumerate(pieces(side, most)):
            src, dst = (
                ref.at[m, side, q, top:bottom, first:end] for ref in (own, got)
            )
            copies.append(
                pltpu.make_async_remote_copy(
                    src_ref=src, dst_ref=dst,
                    send_sem=send_sem.at[m, side, q, i],
                    recv_sem=recv_sem.at[m, side, q, i],
                    device_id=(before if side == LEFT else after, mine),
                    device_id_type=MESH,
                )
            )
        return copies

    def whole():
        return pltpu.make_async_remote_copy(
            src_ref=own.at[0, RIGHT, VIA], dst_ref=got.at[0, RIGHT, VIA],
            send_sem=send_sem.at[0, RIGHT, VIA, 0],
            recv_sem=recv_sem.at[0, RIGHT, VIA, 0],
            device_id=(before, mine), device_id_type=MESH,
        )

    def start(copies):
        for copy in copies:
            copy.start()

    def take(copies):
        for copy in copies:
            copy.wait_recv()

    def drain(copies):
        for copy in copies:
            copy.wait_send()

    def if_goes(side, action):
        pl.when(has_before if side == LEFT else has_after)(action)

    def if_comes(side, action):
        pl.when(has_after if side == LEFT else has_before)(action)

    small = [
        pltpu.make_async_copy(src, dst, small_sem.at[i])
        for i, (src, dst) in enumerate(
            ((off_hbm, off_ref), (pairs_hbm, pairs_ref), (ker_hbm, ker_ref))
        )
    ]
    barrier = pltpu.get_barrier_semaphore()

    def greet(device):
        pl.semaphore_signal(barrier, inc=1, device_id=device, device_id_type=MESH)

    small[0].start()
    load(1, 0).start()
    if_goes(LEFT, lambda: greet((before, mine)))
    if_goes(RIGHT, lambda: greet((after, mine)))
    pl.when(is_source)(lambda: greet((via, mine)))
    pl.when(is_target)(lambda: greet((last, mine)))
    for d in range(1, n_slab):
        peer = lax.rem(mine + d, n_slab)
        greet((me, peer))
    for q in range(1, QUARTERS):
        load(1, q).start()
    for q in range(QUARTERS):
        load(0, q).start()
    small[1].start()
    small[2].start()

    small[0].wait()
    lane = lax.broadcasted_iota(jnp.int32, (BLOCK, BLOCK), 1)
    line = lax.broadcasted_iota(jnp.int32, (BLOCK, BLOCK), 0)

    def shifts_of(block):
        across_lanes = jnp.broadcast_to(
            off_ref[pl.ds(block, 1), :] - BSTEP * block, (BLOCK, BLOCK)
        )
        return across_lanes, jnp.transpose(across_lanes)

    def sorter_of(across_lanes, down_rows):
        ahead = (down_rows < across_lanes) | ((down_rows == across_lanes) & (line < lane))
        place_of = jnp.sum(ahead.astype(jnp.float32), axis=0, keepdims=True)
        return (place_of == line.astype(jnp.float32)).astype(jnp.float32)

    across_lanes, down_rows = shifts_of(me)
    shift[...] = down_rows
    one_hot = sorter_of(across_lanes, down_rows)
    sorter[1, :, :BLOCK] = one_hot.astype(jnp.bfloat16)
    sorter[1, :, BLOCK:] = one_hot.astype(jnp.bfloat16)
    sorted_rows = jnp.sum(one_hot * across_lanes.astype(jnp.float32), axis=1, keepdims=True)
    sorted_shift[...] = jnp.broadcast_to(sorted_rows, (BLOCK, BLOCK)).astype(jnp.int32)

    def place_chunk(m, q):
        high, low = split_rows(x_in[m, q])
        planes = jnp.dot(
            sorter[1], jnp.concatenate([high, low], axis=0),
            preferred_element_type=jnp.float32,
        )
        left, right = place(planes, sorted_shift[...], lane)
        for side, tiles in ((LEFT, left), (RIGHT, right)):
            for i, tile in enumerate(tiles):
                own[m, side, q, :, i * 128 : (i + 1) * 128] = tile

    def split_own(m, q):
        for side in (LEFT, RIGHT):
            high, low = split_rows(own[m, side, q])
            own_b[m, side, q, :BLOCK, :] = high
            own_b[m, side, q, BLOCK:, :] = low

    def send_both(m, q):
        if_goes(LEFT, lambda: start(send(m, LEFT, q)))
        if_goes(RIGHT, lambda: start(send(m, RIGHT, q)))

    load(1, 0).wait()
    place_chunk(1, 0)
    pl.semaphore_wait(
        barrier,
        n_slab - 1 + has_before.astype(jnp.int32) + has_after.astype(jnp.int32)
        + (2 * flows - (far > 0)) * is_relay.astype(jnp.int32)
        + is_stop.astype(jnp.int32),
    )

    def ready(i):
        pl.semaphore_signal(
            ready_sem, inc=1, device_id=(i * ROW + ROW - 1, mine), device_id_type=MESH
        )


    @pl.when(is_relay)
    def _():
        for i in range(flows):
            if i != far:
                ready(i)

    if far > 0:
        pl.when(is_stop)(lambda: ready(far))

    send_both(1, 0)

    def first_step(q, carry):
        load(1, q).wait()
        place_chunk(1, q)
        send_both(1, q)
        return carry

    lax.fori_loop(1, QUARTERS, first_step, 0)

    def blank(q, carry):
        for side in (LEFT, RIGHT):
            comes = has_after if side == LEFT else has_before

            @pl.when(jnp.logical_not(comes))
            def _():
                for m in range(2):
                    got[m, side, q] = jnp.zeros((BLOCK, CHUNK), jnp.float32)

            if most < BLOCK:

                @pl.when(comes)
                def _():
                    for m in range(2):
                        gap = jnp.zeros((BLOCK - most, 128), jnp.float32)
                        if side == LEFT:
                            got[m, side, q, most:, :128] = gap
                        elif m == 1:
                            got[m, side, q, : BLOCK - most, CHUNK - 128 :] = gap
                        else:

                            @pl.when(jnp.logical_not(is_target & (q == VIA)))
                            def _():
                                got[0, side, q, : BLOCK - most, CHUNK - 128 :] = gap

        return carry

    def other_sorters():
        for k, block in ((0, before), (2, after)):
            sorter[k, :, :BLOCK] = sorter_of(*shifts_of(block)).astype(jnp.bfloat16)

    windows = off_ref[...] - BSTEP * lax.broadcasted_iota(jnp.int32, (n_orb, BLOCK), 0)
    excess = jnp.zeros((n_orb, 1), jnp.float32)
    for inside in (windows < TILE, windows > SPREAD - TILE):
        count = jnp.sum(inside.astype(jnp.float32), axis=1, keepdims=True)
        excess = jnp.maximum(excess, count - most)
    over_ref[...] = jnp.broadcast_to(
        jnp.max(excess, axis=0, keepdims=True), (8, 128)
    ).astype(jnp.int32)

    lax.fori_loop(0, QUARTERS, blank, 0)
    other_sorters()
    small[1].wait()
    small[2].wait()

    def across(a, b):
        return lax.dot_general(
            a, b, (((1,), (1,)), ((), ())), preferred_element_type=jnp.float32
        )

    def listed(k):
        return jnp.broadcast_to(
            pairs_ref[0:1, k : k + 1].astype(jnp.float32), (BLOCK, BLOCK)
        )

    for k in range(3):
        high, low = split_rows(ker_ref[0, k] * listed(k))
        both = across(jnp.concatenate([high, low], axis=0), sorter[k, :, :BLOCK])
        for j in range(2):
            mats[k, 1, :, j * BLOCK : (j + 1) * BLOCK] = both.astype(jnp.bfloat16)
        hacc[k] = jnp.zeros((2 * BLOCK, 2 * BLOCK), jnp.float32)

    def second_step(q, carry):
        load(0, q).wait()
        place_chunk(0, q)
        split_own(1, q)
        split_own(0, q)
        for side in (LEFT, RIGHT):
            hacc[1] += across(own_b[0, side, q], own_b[1, side, q])
        return carry

    lax.fori_loop(0, QUARTERS, second_step, 0)

    slots = ((2, (1,)), (0, (0, 2)))

    def spread(group, d):
        first, ks = slots[group]
        peer = lax.rem(mine + d, n_slab)
        there = pl.ds(pl.multiple_of(peer * rows, rows), rows)
        return pltpu.make_async_remote_copy(
            src_ref=hpart.at[first : first + len(ks), there, :],
            dst_ref=hin.at[d, first : first + len(ks)],
            send_sem=rs_send.at[group, d], recv_sem=rs_recv.at[group, d],
            device_id=(me, peer), device_id_type=MESH,
        )

    def share(group, d):
        first, ks = slots[group]
        peer = lax.rem(mine + d, n_slab)
        here = pl.ds(pl.multiple_of(mine * rows, rows), rows)
        part = hsum.at[first : first + len(ks), here, :]
        return pltpu.make_async_remote_copy(
            src_ref=part, dst_ref=part,
            send_sem=ag_send.at[group, d], recv_sem=ag_recv.at[group, d],
            device_id=(me, peer), device_id_type=MESH,
        )

    def reduce_terms(group):
        first, ks = slots[group]
        for i, k in enumerate(ks):
            square = fold(hacc[k])
            hpart[first + i] = square[:, :BLOCK] + square[:, BLOCK:]
        for d in range(1, n_slab):
            spread(group, d).start()

    def reduce_sums(group):
        first, ks = slots[group]
        mine_rows = pl.ds(pl.multiple_of(mine * rows, rows), rows)
        piece = hpart[first : first + len(ks), mine_rows, :]
        for d in range(1, n_slab):
            spread(group, d).wait_recv()
            piece += hin[d, first : first + len(ks)]
        hsum[first : first + len(ks), mine_rows, :] = piece
        for d in range(1, n_slab):
            share(group, d).start()

    volume = 1.0 / math.sqrt(SEG)

    def finish_sums(group):
        first, ks = slots[group]
        for d in range(1, n_slab):
            share(group, d).wait_recv()
        for i, k in enumerate(ks):
            high, low = split_rows(hsum[first + i] * (-volume * listed(k)))
            both = lax.dot_general(
                sorter[1, :, :BLOCK], jnp.concatenate([high, low], axis=1),
                (((0,), (0,)), ((), ())), preferred_element_type=jnp.float32,
            ).astype(jnp.bfloat16)
            for j in range(2):
                mats[k, 0, :BLOCK, j * BLOCK : (j + 1) * BLOCK] = both[:, :BLOCK]
                mats[k, 0, BLOCK:, j * BLOCK : (j + 1) * BLOCK] = both[:, BLOCK:]

    def times(k, m, stack):
        return fold(jnp.dot(mats[k, m], stack, preferred_element_type=jnp.float32))

    reduce_terms(0)

    @pl.when(is_source)
    def _():
        pl.semaphore_wait(ready_sem, 1)
        detour().start()

    def split_got(m, side, q):
        high, low = split_rows(got[m, side, q])
        got_b[m, side, q, :BLOCK, :] = high
        got_b[m, side, q, BLOCK:, :] = low

    def third_step(q, carry):
        for side in (LEFT, RIGHT):
            if_comes(side, lambda: take(send(1, side, q)))
        if_goes(LEFT, lambda: start(send(0, LEFT, q)))
        straight = jnp.logical_not(jnp.logical_and(is_source, q == VIA))
        pl.when(jnp.logical_and(has_after, straight))(
            lambda: start(send(0, RIGHT, q))
        )

        @pl.when(jnp.logical_and(is_relay, q == VIA - 1))
        def _():
            for i in range(flows):
                if i != far:
                    arrived(i).wait_recv()
                    onward(i).start()

        if far > 0:

            @pl.when(jnp.logical_and(is_stop, q == VIA - 2))
            def _():
                arrived(far).wait_recv()
                second_hop().start()

            @pl.when(jnp.logical_and(is_relay, q == VIA))
            def _():
                arrived(far).wait_recv()
                onward(far).start()

        for side in (LEFT, RIGHT):
            split_got(1, side, q)
            hacc[2 - 2 * side] += across(own_b[0, 1 - side, q], got_b[1, side, q])
            total[1 - side, q] = times(2 - 2 * side, 1, got_b[1, side, q])
        pl.when(q == 1)(lambda: reduce_sums(0))
        return carry

    lax.fori_loop(0, QUARTERS, third_step, 0)

    reduce_terms(1)
    finish_sums(0)

    def own_step(q, carry):
        for side in (LEFT, RIGHT):
            total[side, q] += times(1, 0, own_b[0, side, q])
        return carry

    lax.fori_loop(0, QUARTERS, own_step, 0)
    reduce_sums(1)

    def kernel_step(q, carry):
        for side in (LEFT, RIGHT):
            total[side, q] += times(1, 1, own_b[1, side, q])
        return carry

    lax.fori_loop(0, QUARTERS, kernel_step, 0)
    finish_sums(1)

    def take_last(side, q):
        if side == LEFT:
            if_comes(LEFT, lambda: take(send(0, LEFT, q)))
        else:
            around = jnp.logical_and(is_target, q == VIA)
            pl.when(around)(lambda: whole().wait_recv())
            pl.when(jnp.logical_and(has_before, jnp.logical_not(around)))(
                lambda: take(send(0, RIGHT, q))
            )

    def last_step(q, carry):
        sums = []
        for side in (LEFT, RIGHT):
            take_last(1 - side, q)
            split_got(0, 1 - side, q)
            sums.append(total[side, q] + times(2 * side, 0, got_b[0, 1 - side, q]))
        halves = [
            sums[side][:, t * 128 : (t + 1) * 128]
            for side in (LEFT, RIGHT)
            for t in range(TILES)
        ]
        for i, tile in enumerate(pick(halves, shift[...], lane)):
            at = pl.multiple_of(q * CHUNK_IN + i * 128, 128)
            out_ref[:, pl.ds(at, 128)] = tile
        return carry

    lax.fori_loop(0, QUARTERS, last_step, 0)

    @pl.when(is_relay)
    def _():
        for i in range(flows):
            onward(i).wait_send()

    if far > 0:
        pl.when(is_stop)(lambda: second_hop().wait_send())

    for group in range(2):
        for d in range(1, n_slab):
            spread(group, d).wait_send()
            share(group, d).wait_send()
    for q in range(QUARTERS):
        for m in range(2):
            if_goes(LEFT, lambda: drain(send(m, LEFT, q)))
            if (m, q) == (0, VIA):
                pl.when(is_source)(lambda: whole().wait_send())
                pl.when(jnp.logical_and(has_after, jnp.logical_not(is_source)))(
                    lambda: drain(send(m, RIGHT, q))
                )
            else:
                if_goes(RIGHT, lambda: drain(send(m, RIGHT, q)))


def per_device(n_orb, n_slab, orbitals, offsets, pairs, kernel):
    f32, b16 = jnp.float32, jnp.bfloat16
    dma = pltpu.SemaphoreType.DMA
    hbm = pl.BlockSpec(memory_space=pltpu.HBM)
    vmem = pl.BlockSpec(memory_space=pltpu.VMEM)
    operands = (orbitals, offsets.reshape(n_orb, BLOCK), pairs, kernel)

    def call(most, number):
        return pl.pallas_call(
            functools.partial(body, n_orb, n_slab, most),
            out_shape=(
                pltpu.VMEM((BLOCK, QUARTERS * CHUNK_IN), f32),
                pltpu.VMEM((8, 128), jnp.int32),
            ),
            in_specs=[hbm] * 4,
            out_specs=(vmem, vmem),
            scratch_shapes=[
                pltpu.VMEM((n_orb, BLOCK), jnp.int32),
                pltpu.VMEM(pairs.shape, jnp.int32),
                pltpu.VMEM(kernel.shape, f32),
                pltpu.VMEM((2, QUARTERS, BLOCK, CHUNK_IN), f32),
                pltpu.VMEM((2, 2, QUARTERS, BLOCK, CHUNK), f32),
                pltpu.VMEM((2, 2, QUARTERS, BLOCK, CHUNK), f32),
                pltpu.VMEM((2, 2, QUARTERS, 2 * BLOCK, CHUNK), b16),
                pltpu.VMEM((2, 2, QUARTERS, 2 * BLOCK, CHUNK), b16),
                pltpu.VMEM((BLOCK, BLOCK), jnp.int32),
                pltpu.VMEM((BLOCK, BLOCK), jnp.int32),
                pltpu.VMEM((3, BLOCK, 2 * BLOCK), b16),
                pltpu.VMEM((3, 2 * BLOCK, 2 * BLOCK), f32),
                pltpu.VMEM((3, BLOCK, BLOCK), f32),
                pltpu.VMEM((n_slab, 3, BLOCK // n_slab, BLOCK), f32),
                pltpu.VMEM((3, BLOCK, BLOCK), f32),
                pltpu.VMEM((3, 2, 2 * BLOCK, 2 * BLOCK), b16),
                pltpu.VMEM((2, QUARTERS, BLOCK, CHUNK), f32),
                dma((2, QUARTERS)), dma((2, 2, QUARTERS, 2)), dma((2, 2, QUARTERS, 2)),
                dma((2, n_slab)), dma((2, n_slab)), dma((2, n_slab)), dma((2, n_slab)),
                dma((3,)),
                pltpu.VMEM((n_orb // ROW - 1, BLOCK, CHUNK), f32),
                dma((n_orb // ROW - 1,)), dma((n_orb // ROW - 1,)),
                pltpu.SemaphoreType.REGULAR,
            ],
            compiler_params=pltpu.CompilerParams(
                collective_id=number, has_side_effects=True,
                vmem_limit_bytes=40 * 2**20,
            ),
            cost_estimate=pl.CostEstimate(
                flops=2400 * 10**6, bytes_accessed=4 * 2**20, transcendentals=0
            ),
        )(*(pltpu.with_memory_space_constraint(x, pltpu.HBM) for x in operands))

    result, over = call(MOST_ROWS, 0)
    return lax.cond(over[0, 0] > 0, lambda: call(BLOCK, 1)[0], lambda: result)


def solution(mesh):
    n_orb, n_slab = mesh.shape["orb"], mesh.shape["slab"]
    placed = (P(None, "orb", "slab"), P(), P("orb", None), P("orb", None, None, None))
    return jax.shard_map(
        functools.partial(per_device, n_orb, n_slab), mesh=mesh, in_specs=placed,
        out_specs=P("orb", "slab"), check_vma=False,
    )
```

```python
import functools
import math

import jax
import jax.numpy as jnp
from jax import lax
from jax.experimental import pallas as pl
from jax.experimental.pallas import tpu as pltpu
from jax.sharding import PartitionSpec as P

BLOCK = 128
PATCH = 256
SPREAD = 128
BSTEP = 192
SEG = 16384
QUARTERS = 4
PLANES = 2
CHUNK_IN = PLANES * PATCH
TILE = 64
TILES = BSTEP // TILE
CHUNK = PLANES * BSTEP
MOST_ROWS = 88
MESH = pl.DeviceIdType.MESH
LEFT, RIGHT = 0, 1
ROW = 8
VIA = QUARTERS - 1


def lane_gather(tile, index):
    return jnp.take_along_axis(tile, index, axis=1, mode="promise_in_bounds")


def split_rows(value):
    high = value.astype(jnp.bfloat16)
    low = (value - high.astype(jnp.float32)).astype(jnp.bfloat16)
    return high, low


def fold(square):
    return square[:BLOCK] + square[BLOCK:]


def place(planes, u, lane):
    merged = []
    for v in range(2):
        vregs = [planes[:, (2 * x + v) * 128 : (2 * x + v + 1) * 128] for x in range(PLANES)]
        row = []
        for s in range(PLANES):
            turned = [
                lane_gather(vregs[x], jnp.bitwise_and(lane + TILE * (s - x) - u, 127))
                for x in range(PLANES)
            ]
            row.append(jnp.where(lane < TILE, turned[0], turned[1]))
        merged.append(row)
    zero = jnp.zeros_like(merged[0][0])
    within = jnp.bitwise_and(lane, TILE - 1) - u
    left, right = [], []
    for t in range(TILES):
        at = within + TILE * t
        near, far = merged[0][t % 2], merged[1][t % 2]
        left.append(jnp.where(at < 0, zero, jnp.where(at < 128, near, far)))
        at = within + TILE * t + BSTEP
        near, far = merged[0][(t + 1) % 2], merged[1][(t + 1) % 2]
        right.append(jnp.where(at < 128, near, jnp.where(at < 256, far, zero)))
    return left, right


def pick(tiles, u, lane):
    column = lane + u
    outs = []
    for x in range(PLANES):
        index = jnp.bitwise_and(column, TILE - 1) + TILE * x
        turned = [lane_gather(tile, index) for tile in tiles]
        for first in (0, 2):
            value = turned[first + 3]
            for t in range(2, -1, -1):
                value = jnp.where(column < TILE * (t + 1), turned[first + t], value)
            outs.append(value)
    return outs


def pieces(side, most):
    if most == BLOCK:
        return ((0, BLOCK, 0, CHUNK),)
    if side == LEFT:
        return ((0, BLOCK, 128, CHUNK), (0, most, 0, 128))
    return ((0, BLOCK, 0, CHUNK - 128), (BLOCK - most, BLOCK, CHUNK - 128, CHUNK))


def body(
    n_orb, n_slab, most, orb_hbm, off_hbm, pairs_hbm, ker_hbm, out_ref, over_ref,
    off_ref, pairs_ref, ker_ref, x_in, own, got, own_b, got_b, shift, sorted_shift, sorter, hacc, hpart, hin, hsum, mats, total,
    in_sem, send_sem, recv_sem, rs_send, rs_recv, ag_send, ag_recv, small_sem,
    held, held_sem, onward_sem, ready_sem,
):
    me = lax.axis_index("orb")
    mine = lax.axis_index("slab")
    has_before = me > 0
    has_after = me < n_orb - 1
    before = jnp.maximum(me - 1, 0)
    after = jnp.minimum(me + 1, n_orb - 1)
    rows = BLOCK // n_slab

    flows = n_orb // ROW - 1
    last = n_orb - 1
    flow_end = lax.rem(me, ROW) == ROW - 1
    is_source = jnp.logical_and(flow_end, me < last)
    is_relay = me == last
    is_target = jnp.logical_and(lax.rem(me, ROW) == 0, me > 0)
    flow = me // ROW
    far = 1 if flows >= 3 else -1
    stop = (far + 1) * ROW + ROW - 1 if flows >= 3 else last
    is_stop = jnp.logical_and(me == stop, stop < last)
    via = jnp.where(flow == far, stop, last)

    def detour():
        return pltpu.make_async_remote_copy(
            src_ref=own.at[0, RIGHT, VIA], dst_ref=held.at[flow],
            send_sem=send_sem.at[0, RIGHT, VIA, 0], recv_sem=held_sem.at[flow],
            device_id=(via, mine), device_id_type=MESH,
        )

    def onward(i):
        return pltpu.make_async_remote_copy(
            src_ref=held.at[i], dst_ref=got.at[0, RIGHT, VIA],
            send_sem=onward_sem.at[i], recv_sem=recv_sem.at[0, RIGHT, VIA, 0],
            device_id=((i + 1) * ROW, mine), device_id_type=MESH,
        )

    def second_hop():
        return pltpu.make_async_remote_copy(
            src_ref=held.at[far], dst_ref=held.at[far],
            send_sem=onward_sem.at[far], recv_sem=held_sem.at[far],
            device_id=(last, mine), device_id_type=MESH,
        )

    def arrived(i):
        return pltpu.make_async_remote_copy(
            src_ref=held.at[i], dst_ref=held.at[i],
            send_sem=onward_sem.at[i], recv_sem=held_sem.at[i],
            device_id=(before, mine), device_id_type=MESH,
        )

    def load(m, q):
        return pltpu.make_async_copy(
            orb_hbm.at[m, :, pl.ds(pl.multiple_of(q * CHUNK_IN, CHUNK_IN), CHUNK_IN)],
            x_in.at[m, q], in_sem.at[m, q],
        )

    def send(m, side, q):
        copies = []
        for i, (top, bottom, first, end) in enumerate(pieces(side, most)):
            src, dst = (
                ref.at[m, side, q, top:bottom, first:end] for ref in (own, got)
            )
            copies.append(
                pltpu.make_async_remote_copy(
                    src_ref=src, dst_ref=dst,
                    send_sem=send_sem.at[m, side, q, i],
                    recv_sem=recv_sem.at[m, side, q, i],
                    device_id=(before if side == LEFT else after, mine),
                    device_id_type=MESH,
                )
            )
        return copies

    def whole():
        return pltpu.make_async_remote_copy(
            src_ref=own.at[0, RIGHT, VIA], dst_ref=got.at[0, RIGHT, VIA],
            send_sem=send_sem.at[0, RIGHT, VIA, 0],
            recv_sem=recv_sem.at[0, RIGHT, VIA, 0],
            device_id=(before, mine), device_id_type=MESH,
        )

    def start(copies):
        for copy in copies:
            copy.start()

    def take(copies):
        for copy in copies:
            copy.wait_recv()

    def drain(copies):
        for copy in copies:
            copy.wait_send()

    def if_goes(side, action):
        pl.when(has_before if side == LEFT else has_after)(action)

    def if_comes(side, action):
        pl.when(has_after if side == LEFT else has_before)(action)

    small = [
        pltpu.make_async_copy(src, dst, small_sem.at[i])
        for i, (src, dst) in enumerate(
            ((off_hbm, off_ref), (pairs_hbm, pairs_ref), (ker_hbm, ker_ref))
        )
    ]
    barrier = pltpu.get_barrier_semaphore()

    def greet(device):
        pl.semaphore_signal(barrier, inc=1, device_id=device, device_id_type=MESH)

    small[0].start()
    load(1, 0).start()
    if_goes(LEFT, lambda: greet((before, mine)))
    if_goes(RIGHT, lambda: greet((after, mine)))
    pl.when(is_source)(lambda: greet((via, mine)))
    pl.when(is_target)(lambda: greet((last, mine)))
    for d in range(1, n_slab):
        peer = lax.rem(mine + d, n_slab)
        greet((me, peer))
    for q in range(1, QUARTERS):
        load(1, q).start()
    for q in range(QUARTERS):
        load(0, q).start()
    small[1].start()
    small[2].start()

    small[0].wait()
    lane = lax.broadcasted_iota(jnp.int32, (BLOCK, BLOCK), 1)
    line = lax.broadcasted_iota(jnp.int32, (BLOCK, BLOCK), 0)

    def shifts_of(block):
        across_lanes = jnp.broadcast_to(
            off_ref[pl.ds(block, 1), :] - BSTEP * block, (BLOCK, BLOCK)
        )
        return across_lanes, jnp.transpose(across_lanes)

    def sorter_of(across_lanes, down_rows):
        ahead = (down_rows < across_lanes) | ((down_rows == across_lanes) & (line < lane))
        place_of = jnp.sum(ahead.astype(jnp.float32), axis=0, keepdims=True)
        return (place_of == line.astype(jnp.float32)).astype(jnp.float32)

    across_lanes, down_rows = shifts_of(me)
    shift[...] = down_rows
    one_hot = sorter_of(across_lanes, down_rows)
    sorter[1, :, :BLOCK] = one_hot.astype(jnp.bfloat16)
    sorter[1, :, BLOCK:] = one_hot.astype(jnp.bfloat16)
    sorted_rows = jnp.sum(one_hot * across_lanes.astype(jnp.float32), axis=1, keepdims=True)
    sorted_shift[...] = jnp.broadcast_to(sorted_rows, (BLOCK, BLOCK)).astype(jnp.int32)

    def place_chunk(m, q):
        high, low = split_rows(x_in[m, q])
        planes = jnp.dot(
            sorter[1], jnp.concatenate([high, low], axis=0),
            preferred_element_type=jnp.float32,
        )
        left, right = place(planes, sorted_shift[...], lane)
        for side, tiles in ((LEFT, left), (RIGHT, right)):
            for i, tile in enumerate(tiles):
                own[m, side, q, :, i * 128 : (i + 1) * 128] = tile

    def split_own(m, q):
        for side in (LEFT, RIGHT):
            high, low = split_rows(own[m, side, q])
            own_b[m, side, q, :BLOCK, :] = high
            own_b[m, side, q, BLOCK:, :] = low

    def send_both(m, q):
        if_goes(LEFT, lambda: start(send(m, LEFT, q)))
        if_goes(RIGHT, lambda: start(send(m, RIGHT, q)))

    load(1, 0).wait()
    place_chunk(1, 0)
    pl.semaphore_wait(
        barrier,
        n_slab - 1 + has_before.astype(jnp.int32) + has_after.astype(jnp.int32)
        + (2 * flows - (far > 0)) * is_relay.astype(jnp.int32)
        + is_stop.astype(jnp.int32),
    )

    def ready(i):
        pl.semaphore_signal(
            ready_sem, inc=1, device_id=(i * ROW + ROW - 1, mine), device_id_type=MESH
        )


    @pl.when(is_relay)
    def _():
        for i in range(flows):
            if i != far:
                ready(i)

    if far > 0:
        pl.when(is_stop)(lambda: ready(far))

    send_both(1, 0)

    def first_step(q, carry):
        load(1, q).wait()
        place_chunk(1, q)
        send_both(1, q)
        return carry

    lax.fori_loop(1, QUARTERS, first_step, 0)

    def blank(q, carry):
        for side in (LEFT, RIGHT):
            comes = has_after if side == LEFT else has_before

            @pl.when(jnp.logical_not(comes))
            def _():
                for m in range(2):
                    got[m, side, q] = jnp.zeros((BLOCK, CHUNK), jnp.float32)

            if most < BLOCK:

                @pl.when(comes)
                def _():
                    for m in range(2):
                        gap = jnp.zeros((BLOCK - most, 128), jnp.float32)
                        if side == LEFT:
                            got[m, side, q, most:, :128] = gap
                        elif m == 1:
                            got[m, side, q, : BLOCK - most, CHUNK - 128 :] = gap
                        else:

                            @pl.when(jnp.logical_not(is_target & (q == VIA)))
                            def _():
                                got[0, side, q, : BLOCK - most, CHUNK - 128 :] = gap

        return carry

    def other_sorters():
        for k, block in ((0, before), (2, after)):
            sorter[k, :, :BLOCK] = sorter_of(*shifts_of(block)).astype(jnp.bfloat16)

    windows = off_ref[...] - BSTEP * lax.broadcasted_iota(jnp.int32, (n_orb, BLOCK), 0)
    excess = jnp.zeros((n_orb, 1), jnp.float32)
    for inside in (windows < TILE, windows > SPREAD - TILE):
        count = jnp.sum(inside.astype(jnp.float32), axis=1, keepdims=True)
        excess = jnp.maximum(excess, count - most)
    over_ref[0, 0] = jnp.max(excess).astype(jnp.int32)

    lax.fori_loop(0, QUARTERS, blank, 0)
    other_sorters()
    small[1].wait()
    small[2].wait()

    def across(a, b):
        return lax.dot_general(
            a, b, (((1,), (1,)), ((), ())), preferred_element_type=jnp.float32
        )

    def listed(k):
        return jnp.broadcast_to(
            pairs_ref[0:1, k : k + 1].astype(jnp.float32), (BLOCK, BLOCK)
        )

    for k in range(3):
        high, low = split_rows(ker_ref[0, k] * listed(k))
        both = across(jnp.concatenate([high, low], axis=0), sorter[k, :, :BLOCK])
        for j in range(2):
            mats[k, 1, :, j * BLOCK : (j + 1) * BLOCK] = both.astype(jnp.bfloat16)
        hacc[k] = jnp.zeros((2 * BLOCK, 2 * BLOCK), jnp.float32)

    def second_step(q, carry):
        load(0, q).wait()
        place_chunk(0, q)
        split_own(1, q)
        split_own(0, q)
        for side in (LEFT, RIGHT):
            hacc[1] += across(own_b[0, side, q], own_b[1, side, q])
        return carry

    lax.fori_loop(0, QUARTERS, second_step, 0)

    slots = ((2, (1,)), (0, (0, 2)))

    def spread(group, d):
        first, ks = slots[group]
        peer = lax.rem(mine + d, n_slab)
        there = pl.ds(pl.multiple_of(peer * rows, rows), rows)
        return pltpu.make_async_remote_copy(
            src_ref=hpart.at[first : first + len(ks), there, :],
            dst_ref=hin.at[d, first : first + len(ks)],
            send_sem=rs_send.at[group, d], recv_sem=rs_recv.at[group, d],
            device_id=(me, peer), device_id_type=MESH,
        )

    def share(group, d):
        first, ks = slots[group]
        peer = lax.rem(mine + d, n_slab)
        here = pl.ds(pl.multiple_of(mine * rows, rows), rows)
        part = hsum.at[first : first + len(ks), here, :]
        return pltpu.make_async_remote_copy(
            src_ref=part, dst_ref=part,
            send_sem=ag_send.at[group, d], recv_sem=ag_recv.at[group, d],
            device_id=(me, peer), device_id_type=MESH,
        )

    def reduce_terms(group):
        first, ks = slots[group]
        for i, k in enumerate(ks):
            square = fold(hacc[k])
            hpart[first + i] = square[:, :BLOCK] + square[:, BLOCK:]
        for d in range(1, n_slab):
            spread(group, d).start()

    def reduce_sums(group):
        first, ks = slots[group]
        mine_rows = pl.ds(pl.multiple_of(mine * rows, rows), rows)
        piece = hpart[first : first + len(ks), mine_rows, :]
        for d in range(1, n_slab):
            spread(group, d).wait_recv()
            piece += hin[d, first : first + len(ks)]
        hsum[first : first + len(ks), mine_rows, :] = piece
        for d in range(1, n_slab):
            share(group, d).start()

    volume = 1.0 / math.sqrt(SEG)

    def finish_sums(group):
        first, ks = slots[group]
        for d in range(1, n_slab):
            share(group, d).wait_recv()
        for i, k in enumerate(ks):
            high, low = split_rows(hsum[first + i] * (-volume * listed(k)))
            both = lax.dot_general(
                sorter[1, :, :BLOCK], jnp.concatenate([high, low], axis=1),
                (((0,), (0,)), ((), ())), preferred_element_type=jnp.float32,
            ).astype(jnp.bfloat16)
            for j in range(2):
                mats[k, 0, :BLOCK, j * BLOCK : (j + 1) * BLOCK] = both[:, :BLOCK]
                mats[k, 0, BLOCK:, j * BLOCK : (j + 1) * BLOCK] = both[:, BLOCK:]

    def times(k, m, stack):
        return fold(jnp.dot(mats[k, m], stack, preferred_element_type=jnp.float32))

    reduce_terms(0)

    @pl.when(is_source)
    def _():
        pl.semaphore_wait(ready_sem, 1)
        detour().start()

    def split_got(m, side, q):
        high, low = split_rows(got[m, side, q])
        got_b[m, side, q, :BLOCK, :] = high
        got_b[m, side, q, BLOCK:, :] = low

    def third_step(q, carry):
        for side in (LEFT, RIGHT):
            if_comes(side, lambda: take(send(1, side, q)))
        if_goes(LEFT, lambda: start(send(0, LEFT, q)))
        straight = jnp.logical_not(jnp.logical_and(is_source, q == VIA))
        pl.when(jnp.logical_and(has_after, straight))(
            lambda: start(send(0, RIGHT, q))
        )

        @pl.when(jnp.logical_and(is_relay, q == VIA - 1))
        def _():
            for i in range(flows):
                if i != far:
                    arrived(i).wait_recv()
                    onward(i).start()

        if far > 0:

            @pl.when(jnp.logical_and(is_stop, q == VIA - 2))
            def _():
                arrived(far).wait_recv()
                second_hop().start()

            @pl.when(jnp.logical_and(is_relay, q == VIA))
            def _():
                arrived(far).wait_recv()
                onward(far).start()

        for side in (LEFT, RIGHT):
            split_got(1, side, q)
            hacc[2 - 2 * side] += across(own_b[0, 1 - side, q], got_b[1, side, q])
            total[1 - side, q] = times(2 - 2 * side, 1, got_b[1, side, q])
        pl.when(q == 1)(lambda: reduce_sums(0))
        return carry

    lax.fori_loop(0, QUARTERS, third_step, 0)

    reduce_terms(1)
    finish_sums(0)

    def own_step(q, carry):
        for side in (LEFT, RIGHT):
            total[side, q] += times(1, 0, own_b[0, side, q])
        return carry

    lax.fori_loop(0, QUARTERS, own_step, 0)
    reduce_sums(1)

    def kernel_step(q, carry):
        for side in (LEFT, RIGHT):
            total[side, q] += times(1, 1, own_b[1, side, q])
        return carry

    lax.fori_loop(0, QUARTERS, kernel_step, 0)
    finish_sums(1)

    def take_last(side, q):
        if side == LEFT:
            if_comes(LEFT, lambda: take(send(0, LEFT, q)))
        else:
            around = jnp.logical_and(is_target, q == VIA)
            pl.when(around)(lambda: whole().wait_recv())
            pl.when(jnp.logical_and(has_before, jnp.logical_not(around)))(
                lambda: take(send(0, RIGHT, q))
            )

    def last_step(q, carry):
        sums = []
        for side in (LEFT, RIGHT):
            take_last(1 - side, q)
            split_got(0, 1 - side, q)
            sums.append(total[side, q] + times(2 * side, 0, got_b[0, 1 - side, q]))
        halves = [
            sums[side][:, t * 128 : (t + 1) * 128]
            for side in (LEFT, RIGHT)
            for t in range(TILES)
        ]
        for i, tile in enumerate(pick(halves, shift[...], lane)):
            at = pl.multiple_of(q * CHUNK_IN + i * 128, 128)
            out_ref[:, pl.ds(at, 128)] = tile
        return carry

    lax.fori_loop(0, QUARTERS, last_step, 0)

    @pl.when(is_relay)
    def _():
        for i in range(flows):
            onward(i).wait_send()

    if far > 0:
        pl.when(is_stop)(lambda: second_hop().wait_send())

    for group in range(2):
        for d in range(1, n_slab):
            spread(group, d).wait_send()
            share(group, d).wait_send()
    for q in range(QUARTERS):
        for m in range(2):
            if_goes(LEFT, lambda: drain(send(m, LEFT, q)))
            if (m, q) == (0, VIA):
                pl.when(is_source)(lambda: whole().wait_send())
                pl.when(jnp.logical_and(has_after, jnp.logical_not(is_source)))(
                    lambda: drain(send(m, RIGHT, q))
                )
            else:
                if_goes(RIGHT, lambda: drain(send(m, RIGHT, q)))


def per_device(n_orb, n_slab, orbitals, offsets, pairs, kernel):
    f32, b16 = jnp.float32, jnp.bfloat16
    dma = pltpu.SemaphoreType.DMA
    hbm = pl.BlockSpec(memory_space=pltpu.HBM)
    vmem = pl.BlockSpec(memory_space=pltpu.VMEM)
    operands = (orbitals, offsets.reshape(n_orb, BLOCK), pairs, kernel)

    def call(most, number):
        return pl.pallas_call(
            functools.partial(body, n_orb, n_slab, most),
            out_shape=(
                pltpu.VMEM((BLOCK, QUARTERS * CHUNK_IN), f32),
                pltpu.SMEM((1, 1), jnp.int32),
            ),
            in_specs=[hbm] * 4,
            out_specs=(vmem, pl.BlockSpec(memory_space=pltpu.SMEM)),
            scratch_shapes=[
                pltpu.VMEM((n_orb, BLOCK), jnp.int32),
                pltpu.VMEM(pairs.shape, jnp.int32),
                pltpu.VMEM(kernel.shape, f32),
                pltpu.VMEM((2, QUARTERS, BLOCK, CHUNK_IN), f32),
                pltpu.VMEM((2, 2, QUARTERS, BLOCK, CHUNK), f32),
                pltpu.VMEM((2, 2, QUARTERS, BLOCK, CHUNK), f32),
                pltpu.VMEM((2, 2, QUARTERS, 2 * BLOCK, CHUNK), b16),
                pltpu.VMEM((2, 2, QUARTERS, 2 * BLOCK, CHUNK), b16),
                pltpu.VMEM((BLOCK, BLOCK), jnp.int32),
                pltpu.VMEM((BLOCK, BLOCK), jnp.int32),
                pltpu.VMEM((3, BLOCK, 2 * BLOCK), b16),
                pltpu.VMEM((3, 2 * BLOCK, 2 * BLOCK), f32),
                pltpu.VMEM((3, BLOCK, BLOCK), f32),
                pltpu.VMEM((n_slab, 3, BLOCK // n_slab, BLOCK), f32),
                pltpu.VMEM((3, BLOCK, BLOCK), f32),
                pltpu.VMEM((3, 2, 2 * BLOCK, 2 * BLOCK), b16),
                pltpu.VMEM((2, QUARTERS, BLOCK, CHUNK), f32),
                dma((2, QUARTERS)), dma((2, 2, QUARTERS, 2)), dma((2, 2, QUARTERS, 2)),
                dma((2, n_slab)), dma((2, n_slab)), dma((2, n_slab)), dma((2, n_slab)),
                dma((3,)),
                pltpu.VMEM((n_orb // ROW - 1, BLOCK, CHUNK), f32),
                dma((n_orb // ROW - 1,)), dma((n_orb // ROW - 1,)),
                pltpu.SemaphoreType.REGULAR,
            ],
            compiler_params=pltpu.CompilerParams(
                collective_id=number, has_side_effects=True,
                vmem_limit_bytes=40 * 2**20,
            ),
            cost_estimate=pl.CostEstimate(
                flops=2400 * 10**6, bytes_accessed=4 * 2**20, transcendentals=0
            ),
        )(*(pltpu.with_memory_space_constraint(x, pltpu.HBM) for x in operands))

    result, over = call(MOST_ROWS, 0)
    return lax.cond(over.reshape(()) > 0, lambda: call(BLOCK, 1)[0], lambda: result)


def solution(mesh):
    n_orb, n_slab = mesh.shape["orb"], mesh.shape["slab"]
    placed = (P(None, "orb", "slab"), P(), P("orb", None), P("orb", None, None, None))
    return jax.shard_map(
        functools.partial(per_device, n_orb, n_slab), mesh=mesh, in_specs=placed,
        out_specs=P("orb", "slab"), check_vma=False,
    )
```

```python
import functools
import math

import jax
import jax.numpy as jnp
from jax import lax
from jax.experimental import pallas as pl
from jax.experimental.pallas import tpu as pltpu
from jax.sharding import PartitionSpec as P

BLOCK = 128
PATCH = 256
SPREAD = 128
BSTEP = 192
SEG = 16384
QUARTERS = 4
PLANES = 2
CHUNK_IN = PLANES * PATCH
TILE = 64
TILES = BSTEP // TILE
CHUNK = PLANES * BSTEP
MOST_ROWS = 88
MESH = pl.DeviceIdType.MESH
LEFT, RIGHT = 0, 1
ROW = 8
VIA = QUARTERS - 1


def lane_gather(tile, index):
    return jnp.take_along_axis(tile, index, axis=1, mode="promise_in_bounds")


def split_rows(value):
    high = value.astype(jnp.bfloat16)
    low = (value - high.astype(jnp.float32)).astype(jnp.bfloat16)
    return high, low


def fold(square):
    return square[:BLOCK] + square[BLOCK:]


def place(planes, u, lane):
    merged = []
    for v in range(2):
        vregs = [planes[:, (2 * x + v) * 128 : (2 * x + v + 1) * 128] for x in range(PLANES)]
        row = []
        for s in range(PLANES):
            turned = [
                lane_gather(vregs[x], jnp.bitwise_and(lane + TILE * (s - x) - u, 127))
                for x in range(PLANES)
            ]
            row.append(jnp.where(lane < TILE, turned[0], turned[1]))
        merged.append(row)
    zero = jnp.zeros_like(merged[0][0])
    within = jnp.bitwise_and(lane, TILE - 1) - u
    left, right = [], []
    for t in range(TILES):
        at = within + TILE * t
        near, far = merged[0][t % 2], merged[1][t % 2]
        left.append(jnp.where(at < 0, zero, jnp.where(at < 128, near, far)))
        at = within + TILE * t + BSTEP
        near, far = merged[0][(t + 1) % 2], merged[1][(t + 1) % 2]
        right.append(jnp.where(at < 128, near, jnp.where(at < 256, far, zero)))
    return left, right


def pick(tiles, u, lane):
    column = lane + u
    outs = []
    for x in range(PLANES):
        index = jnp.bitwise_and(column, TILE - 1) + TILE * x
        turned = [lane_gather(tile, index) for tile in tiles]
        for first in (0, 2):
            value = turned[first + 3]
            for t in range(2, -1, -1):
                value = jnp.where(column < TILE * (t + 1), turned[first + t], value)
            outs.append(value)
    return outs


def pieces(side, most):
    if most == BLOCK:
        return ((0, BLOCK, 0, CHUNK),)
    if side == LEFT:
        return ((0, BLOCK, 128, CHUNK), (0, most, 0, 128))
    return ((0, BLOCK, 0, CHUNK - 128), (BLOCK - most, BLOCK, CHUNK - 128, CHUNK))


def body(
    n_orb, n_slab, most, orb_hbm, off_hbm, pairs_hbm, ker_hbm, out_ref, over_ref,
    off_ref, pairs_ref, ker_ref, x_in, own, got, own_b, got_b, shift, sorted_shift, sorter, hacc, hpart, hin, hsum, mats, total,
    in_sem, send_sem, recv_sem, rs_send, rs_recv, ag_send, ag_recv, small_sem,
    held, held_sem, onward_sem, ready_sem, peers_sem,
):
    me = lax.axis_index("orb")
    mine = lax.axis_index("slab")
    has_before = me > 0
    has_after = me < n_orb - 1
    before = jnp.maximum(me - 1, 0)
    after = jnp.minimum(me + 1, n_orb - 1)
    rows = BLOCK // n_slab

    flows = n_orb // ROW - 1
    last = n_orb - 1
    flow_end = lax.rem(me, ROW) == ROW - 1
    is_source = jnp.logical_and(flow_end, me < last)
    is_relay = me == last
    is_target = jnp.logical_and(lax.rem(me, ROW) == 0, me > 0)
    flow = me // ROW
    far = 1 if flows >= 3 else -1
    stop = (far + 1) * ROW + ROW - 1 if flows >= 3 else last
    is_stop = jnp.logical_and(me == stop, stop < last)
    via = jnp.where(flow == far, stop, last)

    def detour():
        return pltpu.make_async_remote_copy(
            src_ref=own.at[0, RIGHT, VIA], dst_ref=held.at[flow],
            send_sem=send_sem.at[0, RIGHT, VIA, 0], recv_sem=held_sem.at[flow],
            device_id=(via, mine), device_id_type=MESH,
        )

    def onward(i):
        return pltpu.make_async_remote_copy(
            src_ref=held.at[i], dst_ref=got.at[0, RIGHT, VIA],
            send_sem=onward_sem.at[i], recv_sem=recv_sem.at[0, RIGHT, VIA, 0],
            device_id=((i + 1) * ROW, mine), device_id_type=MESH,
        )

    def second_hop():
        return pltpu.make_async_remote_copy(
            src_ref=held.at[far], dst_ref=held.at[far],
            send_sem=onward_sem.at[far], recv_sem=held_sem.at[far],
            device_id=(last, mine), device_id_type=MESH,
        )

    def arrived(i):
        return pltpu.make_async_remote_copy(
            src_ref=held.at[i], dst_ref=held.at[i],
            send_sem=onward_sem.at[i], recv_sem=held_sem.at[i],
            device_id=(before, mine), device_id_type=MESH,
        )

    def load(m, q):
        return pltpu.make_async_copy(
            orb_hbm.at[m, :, pl.ds(pl.multiple_of(q * CHUNK_IN, CHUNK_IN), CHUNK_IN)],
            x_in.at[m, q], in_sem.at[m, q],
        )

    def send(m, side, q):
        copies = []
        for i, (top, bottom, first, end) in enumerate(pieces(side, most)):
            src, dst = (
                ref.at[m, side, q, top:bottom, first:end] for ref in (own, got)
            )
            copies.append(
                pltpu.make_async_remote_copy(
                    src_ref=src, dst_ref=dst,
                    send_sem=send_sem.at[m, side, q, i],
                    recv_sem=recv_sem.at[m, side, q, i],
                    device_id=(before if side == LEFT else after, mine),
                    device_id_type=MESH,
                )
            )
        return copies

    def whole():
        return pltpu.make_async_remote_copy(
            src_ref=own.at[0, RIGHT, VIA], dst_ref=got.at[0, RIGHT, VIA],
            send_sem=send_sem.at[0, RIGHT, VIA, 0],
            recv_sem=recv_sem.at[0, RIGHT, VIA, 0],
            device_id=(before, mine), device_id_type=MESH,
        )

    def start(copies):
        for copy in copies:
            copy.start()

    def take(copies):
        for copy in copies:
            copy.wait_recv()

    def drain(copies):
        for copy in copies:
            copy.wait_send()

    def if_goes(side, action):
        pl.when(has_before if side == LEFT else has_after)(action)

    def if_comes(side, action):
        pl.when(has_after if side == LEFT else has_before)(action)

    small = [
        pltpu.make_async_copy(src, dst, small_sem.at[i])
        for i, (src, dst) in enumerate(
            ((off_hbm, off_ref), (pairs_hbm, pairs_ref), (ker_hbm, ker_ref))
        )
    ]
    barrier = pltpu.get_barrier_semaphore()

    def greet(device):
        pl.semaphore_signal(barrier, inc=1, device_id=device, device_id_type=MESH)

    small[0].start()
    load(1, 0).start()
    if_goes(LEFT, lambda: greet((before, mine)))
    if_goes(RIGHT, lambda: greet((after, mine)))
    pl.when(is_source)(lambda: greet((via, mine)))
    pl.when(is_target)(lambda: greet((last, mine)))
    for d in range(1, n_slab):
        peer = lax.rem(mine + d, n_slab)
        pl.when(peer > mine)(lambda: greet((me, peer)))
    for q in range(1, QUARTERS):
        load(1, q).start()
    for q in range(QUARTERS):
        load(0, q).start()
    small[1].start()
    small[2].start()

    small[0].wait()
    lane = lax.broadcasted_iota(jnp.int32, (BLOCK, BLOCK), 1)
    line = lax.broadcasted_iota(jnp.int32, (BLOCK, BLOCK), 0)

    def shifts_of(block):
        across_lanes = jnp.broadcast_to(
            off_ref[pl.ds(block, 1), :] - BSTEP * block, (BLOCK, BLOCK)
        )
        return across_lanes, jnp.transpose(across_lanes)

    def sorter_of(across_lanes, down_rows):
        ahead = (down_rows < across_lanes) | ((down_rows == across_lanes) & (line < lane))
        place_of = jnp.sum(ahead.astype(jnp.float32), axis=0, keepdims=True)
        return (place_of == line.astype(jnp.float32)).astype(jnp.float32)

    across_lanes, down_rows = shifts_of(me)
    shift[...] = down_rows
    one_hot = sorter_of(across_lanes, down_rows)
    sorter[1, :, :BLOCK] = one_hot.astype(jnp.bfloat16)
    sorter[1, :, BLOCK:] = one_hot.astype(jnp.bfloat16)
    sorted_rows = jnp.sum(one_hot * across_lanes.astype(jnp.float32), axis=1, keepdims=True)
    sorted_shift[...] = jnp.broadcast_to(sorted_rows, (BLOCK, BLOCK)).astype(jnp.int32)

    def place_chunk(m, q):
        high, low = split_rows(x_in[m, q])
        planes = jnp.dot(
            sorter[1], jnp.concatenate([high, low], axis=0),
            preferred_element_type=jnp.float32,
        )
        left, right = place(planes, sorted_shift[...], lane)
        for side, tiles in ((LEFT, left), (RIGHT, right)):
            for i, tile in enumerate(tiles):
                own[m, side, q, :, i * 128 : (i + 1) * 128] = tile

    def split_own(m, q):
        for side in (LEFT, RIGHT):
            high, low = split_rows(own[m, side, q])
            own_b[m, side, q, :BLOCK, :] = high
            own_b[m, side, q, BLOCK:, :] = low

    def send_both(m, q):
        if_goes(LEFT, lambda: start(send(m, LEFT, q)))
        if_goes(RIGHT, lambda: start(send(m, RIGHT, q)))

    load(1, 0).wait()
    place_chunk(1, 0)
    pl.semaphore_wait(
        barrier,
        mine + has_before.astype(jnp.int32) + has_after.astype(jnp.int32)
        + (2 * flows - (far > 0)) * is_relay.astype(jnp.int32)
        + is_stop.astype(jnp.int32),
    )

    def ready(i):
        pl.semaphore_signal(
            ready_sem, inc=1, device_id=(i * ROW + ROW - 1, mine), device_id_type=MESH
        )


    @pl.when(is_relay)
    def _():
        for i in range(flows):
            if i != far:
                ready(i)

    if far > 0:
        pl.when(is_stop)(lambda: ready(far))

    send_both(1, 0)

    for d in range(1, n_slab):
        peer = lax.rem(mine + d, n_slab)

        @pl.when(peer < mine)
        def _():
            pl.semaphore_signal(
                peers_sem, inc=1, device_id=(me, peer), device_id_type=MESH
            )

    def first_step(q, carry):
        load(1, q).wait()
        place_chunk(1, q)
        send_both(1, q)
        return carry

    lax.fori_loop(1, QUARTERS, first_step, 0)

    def blank(q, carry):
        for side in (LEFT, RIGHT):
            comes = has_after if side == LEFT else has_before

            @pl.when(jnp.logical_not(comes))
            def _():
                for m in range(2):
                    got[m, side, q] = jnp.zeros((BLOCK, CHUNK), jnp.float32)

            if most < BLOCK:

                @pl.when(comes)
                def _():
                    for m in range(2):
                        gap = jnp.zeros((BLOCK - most, 128), jnp.float32)
                        if side == LEFT:
                            got[m, side, q, most:, :128] = gap
                        elif m == 1:
                            got[m, side, q, : BLOCK - most, CHUNK - 128 :] = gap
                        else:

                            @pl.when(jnp.logical_not(is_target & (q == VIA)))
                            def _():
                                got[0, side, q, : BLOCK - most, CHUNK - 128 :] = gap

        return carry

    def other_sorters():
        for k, block in ((0, before), (2, after)):
            sorter[k, :, :BLOCK] = sorter_of(*shifts_of(block)).astype(jnp.bfloat16)

    windows = off_ref[...] - BSTEP * lax.broadcasted_iota(jnp.int32, (n_orb, BLOCK), 0)
    excess = jnp.zeros((n_orb, 1), jnp.float32)
    for inside in (windows < TILE, windows > SPREAD - TILE):
        count = jnp.sum(inside.astype(jnp.float32), axis=1, keepdims=True)
        excess = jnp.maximum(excess, count - most)
    over_ref[0, 0] = jnp.max(excess).astype(jnp.int32)

    lax.fori_loop(0, QUARTERS, blank, 0)
    other_sorters()
    small[1].wait()
    small[2].wait()

    def across(a, b):
        return lax.dot_general(
            a, b, (((1,), (1,)), ((), ())), preferred_element_type=jnp.float32
        )

    def listed(k):
        return jnp.broadcast_to(
            pairs_ref[0:1, k : k + 1].astype(jnp.float32), (BLOCK, BLOCK)
        )

    for k in range(3):
        high, low = split_rows(ker_ref[0, k] * listed(k))
        both = across(jnp.concatenate([high, low], axis=0), sorter[k, :, :BLOCK])
        for j in range(2):
            mats[k, 1, :, j * BLOCK : (j + 1) * BLOCK] = both.astype(jnp.bfloat16)
        hacc[k] = jnp.zeros((2 * BLOCK, 2 * BLOCK), jnp.float32)

    def second_step(q, carry):
        load(0, q).wait()
        place_chunk(0, q)
        split_own(1, q)
        split_own(0, q)
        for side in (LEFT, RIGHT):
            hacc[1] += across(own_b[0, side, q], own_b[1, side, q])
        return carry

    lax.fori_loop(0, QUARTERS, second_step, 0)

    slots = ((2, (1,)), (0, (0, 2)))

    def spread(group, d):
        first, ks = slots[group]
        peer = lax.rem(mine + d, n_slab)
        there = pl.ds(pl.multiple_of(peer * rows, rows), rows)
        return pltpu.make_async_remote_copy(
            src_ref=hpart.at[first : first + len(ks), there, :],
            dst_ref=hin.at[d, first : first + len(ks)],
            send_sem=rs_send.at[group, d], recv_sem=rs_recv.at[group, d],
            device_id=(me, peer), device_id_type=MESH,
        )

    def share(group, d):
        first, ks = slots[group]
        peer = lax.rem(mine + d, n_slab)
        here = pl.ds(pl.multiple_of(mine * rows, rows), rows)
        part = hsum.at[first : first + len(ks), here, :]
        return pltpu.make_async_remote_copy(
            src_ref=part, dst_ref=part,
            send_sem=ag_send.at[group, d], recv_sem=ag_recv.at[group, d],
            device_id=(me, peer), device_id_type=MESH,
        )

    def reduce_terms(group):
        first, ks = slots[group]
        for i, k in enumerate(ks):
            square = fold(hacc[k])
            hpart[first + i] = square[:, :BLOCK] + square[:, BLOCK:]
        for d in range(1, n_slab):
            spread(group, d).start()

    def reduce_sums(group):
        first, ks = slots[group]
        mine_rows = pl.ds(pl.multiple_of(mine * rows, rows), rows)
        piece = hpart[first : first + len(ks), mine_rows, :]
        for d in range(1, n_slab):
            spread(group, d).wait_recv()
            piece += hin[d, first : first + len(ks)]
        hsum[first : first + len(ks), mine_rows, :] = piece
        for d in range(1, n_slab):
            share(group, d).start()

    volume = 1.0 / math.sqrt(SEG)

    def finish_sums(group):
        first, ks = slots[group]
        for d in range(1, n_slab):
            share(group, d).wait_recv()
        for i, k in enumerate(ks):
            high, low = split_rows(hsum[first + i] * (-volume * listed(k)))
            both = lax.dot_general(
                sorter[1, :, :BLOCK], jnp.concatenate([high, low], axis=1),
                (((0,), (0,)), ((), ())), preferred_element_type=jnp.float32,
            ).astype(jnp.bfloat16)
            for j in range(2):
                mats[k, 0, :BLOCK, j * BLOCK : (j + 1) * BLOCK] = both[:, :BLOCK]
                mats[k, 0, BLOCK:, j * BLOCK : (j + 1) * BLOCK] = both[:, BLOCK:]

    def times(k, m, stack):
        return fold(jnp.dot(mats[k, m], stack, preferred_element_type=jnp.float32))

    pl.when(mine < n_slab - 1)(
        lambda: pl.semaphore_wait(peers_sem, n_slab - 1 - mine)
    )
    reduce_terms(0)

    @pl.when(is_source)
    def _():
        pl.semaphore_wait(ready_sem, 1)
        detour().start()

    def split_got(m, side, q):
        high, low = split_rows(got[m, side, q])
        got_b[m, side, q, :BLOCK, :] = high
        got_b[m, side, q, BLOCK:, :] = low

    def third_step(q, carry):
        for side in (LEFT, RIGHT):
            if_comes(side, lambda: take(send(1, side, q)))
        if_goes(LEFT, lambda: start(send(0, LEFT, q)))
        straight = jnp.logical_not(jnp.logical_and(is_source, q == VIA))
        pl.when(jnp.logical_and(has_after, straight))(
            lambda: start(send(0, RIGHT, q))
        )

        @pl.when(jnp.logical_and(is_relay, q == VIA - 1))
        def _():
            for i in range(flows):
                if i != far:
                    arrived(i).wait_recv()
                    onward(i).start()

        if far > 0:

            @pl.when(jnp.logical_and(is_stop, q == VIA - 2))
            def _():
                arrived(far).wait_recv()
                second_hop().start()

            @pl.when(jnp.logical_and(is_relay, q == VIA))
            def _():
                arrived(far).wait_recv()
                onward(far).start()

        for side in (LEFT, RIGHT):
            split_got(1, side, q)
            hacc[2 - 2 * side] += across(own_b[0, 1 - side, q], got_b[1, side, q])
            total[1 - side, q] = times(2 - 2 * side, 1, got_b[1, side, q])
        pl.when(q == 1)(lambda: reduce_sums(0))
        return carry

    lax.fori_loop(0, QUARTERS, third_step, 0)

    reduce_terms(1)
    finish_sums(0)

    def own_step(q, carry):
        for side in (LEFT, RIGHT):
            total[side, q] += times(1, 0, own_b[0, side, q])
        return carry

    lax.fori_loop(0, QUARTERS, own_step, 0)
    reduce_sums(1)

    def kernel_step(q, carry):
        for side in (LEFT, RIGHT):
            total[side, q] += times(1, 1, own_b[1, side, q])
        return carry

    lax.fori_loop(0, QUARTERS, kernel_step, 0)
    finish_sums(1)

    def take_last(side, q):
        if side == LEFT:
            if_comes(LEFT, lambda: take(send(0, LEFT, q)))
        else:
            around = jnp.logical_and(is_target, q == VIA)
            pl.when(around)(lambda: whole().wait_recv())
            pl.when(jnp.logical_and(has_before, jnp.logical_not(around)))(
                lambda: take(send(0, RIGHT, q))
            )

    def last_step(q, carry):
        sums = []
        for side in (LEFT, RIGHT):
            take_last(1 - side, q)
            split_got(0, 1 - side, q)
            sums.append(total[side, q] + times(2 * side, 0, got_b[0, 1 - side, q]))
        halves = [
            sums[side][:, t * 128 : (t + 1) * 128]
            for side in (LEFT, RIGHT)
            for t in range(TILES)
        ]
        for i, tile in enumerate(pick(halves, shift[...], lane)):
            at = pl.multiple_of(q * CHUNK_IN + i * 128, 128)
            out_ref[:, pl.ds(at, 128)] = tile
        return carry

    lax.fori_loop(0, QUARTERS, last_step, 0)

    @pl.when(is_relay)
    def _():
        for i in range(flows):
            onward(i).wait_send()

    if far > 0:
        pl.when(is_stop)(lambda: second_hop().wait_send())

    for group in range(2):
        for d in range(1, n_slab):
            spread(group, d).wait_send()
            share(group, d).wait_send()
    for q in range(QUARTERS):
        for m in range(2):
            if_goes(LEFT, lambda: drain(send(m, LEFT, q)))
            if (m, q) == (0, VIA):
                pl.when(is_source)(lambda: whole().wait_send())
                pl.when(jnp.logical_and(has_after, jnp.logical_not(is_source)))(
                    lambda: drain(send(m, RIGHT, q))
                )
            else:
                if_goes(RIGHT, lambda: drain(send(m, RIGHT, q)))


def per_device(n_orb, n_slab, orbitals, offsets, pairs, kernel):
    f32, b16 = jnp.float32, jnp.bfloat16
    dma = pltpu.SemaphoreType.DMA
    hbm = pl.BlockSpec(memory_space=pltpu.HBM)
    vmem = pl.BlockSpec(memory_space=pltpu.VMEM)
    operands = (orbitals, offsets.reshape(n_orb, BLOCK), pairs, kernel)

    def call(most, number):
        return pl.pallas_call(
            functools.partial(body, n_orb, n_slab, most),
            out_shape=(
                pltpu.VMEM((BLOCK, QUARTERS * CHUNK_IN), f32),
                pltpu.SMEM((1, 1), jnp.int32),
            ),
            in_specs=[hbm] * 4,
            out_specs=(vmem, pl.BlockSpec(memory_space=pltpu.SMEM)),
            scratch_shapes=[
                pltpu.VMEM((n_orb, BLOCK), jnp.int32),
                pltpu.VMEM(pairs.shape, jnp.int32),
                pltpu.VMEM(kernel.shape, f32),
                pltpu.VMEM((2, QUARTERS, BLOCK, CHUNK_IN), f32),
                pltpu.VMEM((2, 2, QUARTERS, BLOCK, CHUNK), f32),
                pltpu.VMEM((2, 2, QUARTERS, BLOCK, CHUNK), f32),
                pltpu.VMEM((2, 2, QUARTERS, 2 * BLOCK, CHUNK), b16),
                pltpu.VMEM((2, 2, QUARTERS, 2 * BLOCK, CHUNK), b16),
                pltpu.VMEM((BLOCK, BLOCK), jnp.int32),
                pltpu.VMEM((BLOCK, BLOCK), jnp.int32),
                pltpu.VMEM((3, BLOCK, 2 * BLOCK), b16),
                pltpu.VMEM((3, 2 * BLOCK, 2 * BLOCK), f32),
                pltpu.VMEM((3, BLOCK, BLOCK), f32),
                pltpu.VMEM((n_slab, 3, BLOCK // n_slab, BLOCK), f32),
                pltpu.VMEM((3, BLOCK, BLOCK), f32),
                pltpu.VMEM((3, 2, 2 * BLOCK, 2 * BLOCK), b16),
                pltpu.VMEM((2, QUARTERS, BLOCK, CHUNK), f32),
                dma((2, QUARTERS)), dma((2, 2, QUARTERS, 2)), dma((2, 2, QUARTERS, 2)),
                dma((2, n_slab)), dma((2, n_slab)), dma((2, n_slab)), dma((2, n_slab)),
                dma((3,)),
                pltpu.VMEM((n_orb // ROW - 1, BLOCK, CHUNK), f32),
                dma((n_orb // ROW - 1,)), dma((n_orb // ROW - 1,)),
                pltpu.SemaphoreType.REGULAR, pltpu.SemaphoreType.REGULAR,
            ],
            compiler_params=pltpu.CompilerParams(
                collective_id=number, has_side_effects=True,
                vmem_limit_bytes=40 * 2**20,
            ),
            cost_estimate=pl.CostEstimate(
                flops=2400 * 10**6, bytes_accessed=4 * 2**20, transcendentals=0
            ),
        )(*(pltpu.with_memory_space_constraint(x, pltpu.HBM) for x in operands))

    result, over = call(MOST_ROWS, 0)
    return lax.cond(over.reshape(()) > 0, lambda: call(BLOCK, 1)[0], lambda: result)


def solution(mesh):
    n_orb, n_slab = mesh.shape["orb"], mesh.shape["slab"]
    placed = (P(None, "orb", "slab"), P(), P("orb", None), P("orb", None, None, None))
    return jax.shard_map(
        functools.partial(per_device, n_orb, n_slab), mesh=mesh, in_specs=placed,
        out_specs=P("orb", "slab"), check_vma=False,
    )
```

```python
import functools
import math

import jax
import jax.numpy as jnp
from jax import lax
from jax.experimental import pallas as pl
from jax.experimental.pallas import tpu as pltpu
from jax.sharding import PartitionSpec as P

BLOCK = 128
PATCH = 256
SPREAD = 128
BSTEP = 192
SEG = 16384
QUARTERS = 4
PLANES = 2
CHUNK_IN = PLANES * PATCH
TILE = 64
TILES = BSTEP // TILE
CHUNK = PLANES * BSTEP
MOST_ROWS = 88
MESH = pl.DeviceIdType.MESH
LEFT, RIGHT = 0, 1
ROW = 8
VIA = QUARTERS - 2


def lane_gather(tile, index):
    return jnp.take_along_axis(tile, index, axis=1, mode="promise_in_bounds")


def split_rows(value):
    high = value.astype(jnp.bfloat16)
    low = (value - high.astype(jnp.float32)).astype(jnp.bfloat16)
    return high, low


def fold(square):
    return square[:BLOCK] + square[BLOCK:]


def place(planes, u, lane):
    merged = []
    for v in range(2):
        vregs = [planes[:, (2 * x + v) * 128 : (2 * x + v + 1) * 128] for x in range(PLANES)]
        row = []
        for s in range(PLANES):
            turned = [
                lane_gather(vregs[x], jnp.bitwise_and(lane + TILE * (s - x) - u, 127))
                for x in range(PLANES)
            ]
            row.append(jnp.where(lane < TILE, turned[0], turned[1]))
        merged.append(row)
    zero = jnp.zeros_like(merged[0][0])
    within = jnp.bitwise_and(lane, TILE - 1) - u
    left, right = [], []
    for t in range(TILES):
        at = within + TILE * t
        near, far = merged[0][t % 2], merged[1][t % 2]
        left.append(jnp.where(at < 0, zero, jnp.where(at < 128, near, far)))
        at = within + TILE * t + BSTEP
        near, far = merged[0][(t + 1) % 2], merged[1][(t + 1) % 2]
        right.append(jnp.where(at < 128, near, jnp.where(at < 256, far, zero)))
    return left, right


def pick(tiles, u, lane):
    column = lane + u
    outs = []
    for x in range(PLANES):
        index = jnp.bitwise_and(column, TILE - 1) + TILE * x
        turned = [lane_gather(tile, index) for tile in tiles]
        for first in (0, 2):
            value = turned[first + 3]
            for t in range(2, -1, -1):
                value = jnp.where(column < TILE * (t + 1), turned[first + t], value)
            outs.append(value)
    return outs


def pieces(side, most):
    if most == BLOCK:
        return ((0, BLOCK, 0, CHUNK),)
    if side == LEFT:
        return ((0, BLOCK, 128, CHUNK), (0, most, 0, 128))
    return ((0, BLOCK, 0, CHUNK - 128), (BLOCK - most, BLOCK, CHUNK - 128, CHUNK))


def body(
    n_orb, n_slab, most, orb_hbm, off_hbm, pairs_hbm, ker_hbm, out_ref, over_ref,
    off_ref, pairs_ref, ker_ref, x_in, own, got, own_b, got_b, shift, sorted_shift, sorter, hacc, hpart, hin, hsum, mats, total,
    in_sem, send_sem, recv_sem, rs_send, rs_recv, ag_send, ag_recv, small_sem,
    held, held_sem, onward_sem, ready_sem, peers_sem,
):
    me = lax.axis_index("orb")
    mine = lax.axis_index("slab")
    has_before = me > 0
    has_after = me < n_orb - 1
    before = jnp.maximum(me - 1, 0)
    after = jnp.minimum(me + 1, n_orb - 1)
    rows = BLOCK // n_slab

    flows = n_orb // ROW - 1
    last = n_orb - 1
    flow_end = lax.rem(me, ROW) == ROW - 1
    is_source = jnp.logical_and(flow_end, me < last)
    is_relay = me == last
    is_target = jnp.logical_and(lax.rem(me, ROW) == 0, me > 0)
    flow = me // ROW
    far = 1 if flows >= 3 else -1
    stop = (far + 1) * ROW + ROW - 1 if flows >= 3 else last
    is_stop = jnp.logical_and(me == stop, stop < last)
    via = jnp.where(flow == far, stop, last)

    def detour():
        return pltpu.make_async_remote_copy(
            src_ref=own.at[0, RIGHT, VIA], dst_ref=held.at[flow],
            send_sem=send_sem.at[0, RIGHT, VIA, 0], recv_sem=held_sem.at[flow],
            device_id=(via, mine), device_id_type=MESH,
        )

    def onward(i):
        return pltpu.make_async_remote_copy(
            src_ref=held.at[i], dst_ref=got.at[0, RIGHT, VIA],
            send_sem=onward_sem.at[i], recv_sem=recv_sem.at[0, RIGHT, VIA, 0],
            device_id=((i + 1) * ROW, mine), device_id_type=MESH,
        )

    def second_hop():
        return pltpu.make_async_remote_copy(
            src_ref=held.at[far], dst_ref=held.at[far],
            send_sem=onward_sem.at[far], recv_sem=held_sem.at[far],
            device_id=(last, mine), device_id_type=MESH,
        )

    def arrived(i):
        return pltpu.make_async_remote_copy(
            src_ref=held.at[i], dst_ref=held.at[i],
            send_sem=onward_sem.at[i], recv_sem=held_sem.at[i],
            device_id=(before, mine), device_id_type=MESH,
        )

    def load(m, q):
        return pltpu.make_async_copy(
            orb_hbm.at[m, :, pl.ds(pl.multiple_of(q * CHUNK_IN, CHUNK_IN), CHUNK_IN)],
            x_in.at[m, q], in_sem.at[m, q],
        )

    def send(m, side, q):
        copies = []
        for i, (top, bottom, first, end) in enumerate(pieces(side, most)):
            src, dst = (
                ref.at[m, side, q, top:bottom, first:end] for ref in (own, got)
            )
            copies.append(
                pltpu.make_async_remote_copy(
                    src_ref=src, dst_ref=dst,
                    send_sem=send_sem.at[m, side, q, i],
                    recv_sem=recv_sem.at[m, side, q, i],
                    device_id=(before if side == LEFT else after, mine),
                    device_id_type=MESH,
                )
            )
        return copies

    def whole():
        return pltpu.make_async_remote_copy(
            src_ref=own.at[0, RIGHT, VIA], dst_ref=got.at[0, RIGHT, VIA],
            send_sem=send_sem.at[0, RIGHT, VIA, 0],
            recv_sem=recv_sem.at[0, RIGHT, VIA, 0],
            device_id=(before, mine), device_id_type=MESH,
        )

    def start(copies):
        for copy in copies:
            copy.start()

    def take(copies):
        for copy in copies:
            copy.wait_recv()

    def drain(copies):
        for copy in copies:
            copy.wait_send()

    def if_goes(side, action):
        pl.when(has_before if side == LEFT else has_after)(action)

    def if_comes(side, action):
        pl.when(has_after if side == LEFT else has_before)(action)

    small = [
        pltpu.make_async_copy(src, dst, small_sem.at[i])
        for i, (src, dst) in enumerate(
            ((off_hbm, off_ref), (pairs_hbm, pairs_ref), (ker_hbm, ker_ref))
        )
    ]
    barrier = pltpu.get_barrier_semaphore()

    def greet(device):
        pl.semaphore_signal(barrier, inc=1, device_id=device, device_id_type=MESH)

    small[0].start()
    load(1, 0).start()
    if_goes(LEFT, lambda: greet((before, mine)))
    if_goes(RIGHT, lambda: greet((after, mine)))
    pl.when(is_source)(lambda: greet((via, mine)))
    pl.when(is_target)(lambda: greet((last, mine)))
    for d in range(1, n_slab):
        peer = lax.rem(mine + d, n_slab)
        pl.when(peer > mine)(lambda: greet((me, peer)))
    for q in range(1, QUARTERS):
        load(1, q).start()
    for q in range(QUARTERS):
        load(0, q).start()
    small[1].start()
    small[2].start()

    small[0].wait()
    lane = lax.broadcasted_iota(jnp.int32, (BLOCK, BLOCK), 1)
    line = lax.broadcasted_iota(jnp.int32, (BLOCK, BLOCK), 0)

    def shifts_of(block):
        across_lanes = jnp.broadcast_to(
            off_ref[pl.ds(block, 1), :] - BSTEP * block, (BLOCK, BLOCK)
        )
        return across_lanes, jnp.transpose(across_lanes)

    def sorter_of(across_lanes, down_rows):
        ahead = (down_rows < across_lanes) | ((down_rows == across_lanes) & (line < lane))
        place_of = jnp.sum(ahead.astype(jnp.float32), axis=0, keepdims=True)
        return (place_of == line.astype(jnp.float32)).astype(jnp.float32)

    across_lanes, down_rows = shifts_of(me)
    shift[...] = down_rows
    one_hot = sorter_of(across_lanes, down_rows)
    sorter[1, :, :BLOCK] = one_hot.astype(jnp.bfloat16)
    sorter[1, :, BLOCK:] = one_hot.astype(jnp.bfloat16)
    sorted_rows = jnp.sum(one_hot * across_lanes.astype(jnp.float32), axis=1, keepdims=True)
    sorted_shift[...] = jnp.broadcast_to(sorted_rows, (BLOCK, BLOCK)).astype(jnp.int32)

    def place_chunk(m, q):
        high, low = split_rows(x_in[m, q])
        planes = jnp.dot(
            sorter[1], jnp.concatenate([high, low], axis=0),
            preferred_element_type=jnp.float32,
        )
        left, right = place(planes, sorted_shift[...], lane)
        for side, tiles in ((LEFT, left), (RIGHT, right)):
            for i, tile in enumerate(tiles):
                own[m, side, q, :, i * 128 : (i + 1) * 128] = tile

    def split_own(m, q):
        for side in (LEFT, RIGHT):
            high, low = split_rows(own[m, side, q])
            own_b[m, side, q, :BLOCK, :] = high
            own_b[m, side, q, BLOCK:, :] = low

    def send_both(m, q):
        if_goes(LEFT, lambda: start(send(m, LEFT, q)))
        if_goes(RIGHT, lambda: start(send(m, RIGHT, q)))

    load(1, 0).wait()
    place_chunk(1, 0)
    pl.semaphore_wait(
        barrier,
        mine + has_before.astype(jnp.int32) + has_after.astype(jnp.int32)
        + (2 * flows - (far > 0)) * is_relay.astype(jnp.int32)
        + is_stop.astype(jnp.int32),
    )

    def ready(i):
        pl.semaphore_signal(
            ready_sem, inc=1, device_id=(i * ROW + ROW - 1, mine), device_id_type=MESH
        )


    @pl.when(is_relay)
    def _():
        for i in range(flows):
            if i != far:
                ready(i)

    if far > 0:
        pl.when(is_stop)(lambda: ready(far))

    send_both(1, 0)

    for d in range(1, n_slab):
        peer = lax.rem(mine + d, n_slab)

        @pl.when(peer < mine)
        def _():
            pl.semaphore_signal(
                peers_sem, inc=1, device_id=(me, peer), device_id_type=MESH
            )

    def first_step(q, carry):
        load(1, q).wait()
        place_chunk(1, q)
        send_both(1, q)
        return carry

    lax.fori_loop(1, QUARTERS, first_step, 0)

    def blank(q, carry):
        for side in (LEFT, RIGHT):
            comes = has_after if side == LEFT else has_before

            @pl.when(jnp.logical_not(comes))
            def _():
                for m in range(2):
                    got[m, side, q] = jnp.zeros((BLOCK, CHUNK), jnp.float32)

            if most < BLOCK:

                @pl.when(comes)
                def _():
                    for m in range(2):
                        gap = jnp.zeros((BLOCK - most, 128), jnp.float32)
                        if side == LEFT:
                            got[m, side, q, most:, :128] = gap
                        elif m == 1:
                            got[m, side, q, : BLOCK - most, CHUNK - 128 :] = gap
                        else:

                            @pl.when(jnp.logical_not(is_target & (q == VIA)))
                            def _():
                                got[0, side, q, : BLOCK - most, CHUNK - 128 :] = gap

        return carry

    def other_sorters():
        for k, block in ((0, before), (2, after)):
            sorter[k, :, :BLOCK] = sorter_of(*shifts_of(block)).astype(jnp.bfloat16)

    windows = off_ref[...] - BSTEP * lax.broadcasted_iota(jnp.int32, (n_orb, BLOCK), 0)
    excess = jnp.zeros((n_orb, 1), jnp.float32)
    for inside in (windows < TILE, windows > SPREAD - TILE):
        count = jnp.sum(inside.astype(jnp.float32), axis=1, keepdims=True)
        excess = jnp.maximum(excess, count - most)
    over_ref[0, 0] = jnp.max(excess).astype(jnp.int32)

    lax.fori_loop(0, QUARTERS, blank, 0)
    other_sorters()
    small[1].wait()
    small[2].wait()

    def across(a, b):
        return lax.dot_general(
            a, b, (((1,), (1,)), ((), ())), preferred_element_type=jnp.float32
        )

    def listed(k):
        return jnp.broadcast_to(
            pairs_ref[0:1, k : k + 1].astype(jnp.float32), (BLOCK, BLOCK)
        )

    for k in range(3):
        high, low = split_rows(ker_ref[0, k] * listed(k))
        both = across(jnp.concatenate([high, low], axis=0), sorter[k, :, :BLOCK])
        for j in range(2):
            mats[k, 1, :, j * BLOCK : (j + 1) * BLOCK] = both.astype(jnp.bfloat16)
        hacc[k] = jnp.zeros((2 * BLOCK, 2 * BLOCK), jnp.float32)

    def second_step(q, carry):
        load(0, q).wait()
        place_chunk(0, q)
        split_own(1, q)
        split_own(0, q)
        for side in (LEFT, RIGHT):
            hacc[1] += across(own_b[0, side, q], own_b[1, side, q])
        return carry

    lax.fori_loop(0, QUARTERS, second_step, 0)

    slots = ((2, (1,)), (0, (0, 2)))

    def spread(group, d):
        first, ks = slots[group]
        peer = lax.rem(mine + d, n_slab)
        there = pl.ds(pl.multiple_of(peer * rows, rows), rows)
        return pltpu.make_async_remote_copy(
            src_ref=hpart.at[first : first + len(ks), there, :],
            dst_ref=hin.at[d, first : first + len(ks)],
            send_sem=rs_send.at[group, d], recv_sem=rs_recv.at[group, d],
            device_id=(me, peer), device_id_type=MESH,
        )

    def share(group, d):
        first, ks = slots[group]
        peer = lax.rem(mine + d, n_slab)
        here = pl.ds(pl.multiple_of(mine * rows, rows), rows)
        part = hsum.at[first : first + len(ks), here, :]
        return pltpu.make_async_remote_copy(
            src_ref=part, dst_ref=part,
            send_sem=ag_send.at[group, d], recv_sem=ag_recv.at[group, d],
            device_id=(me, peer), device_id_type=MESH,
        )

    def reduce_terms(group):
        first, ks = slots[group]
        for i, k in enumerate(ks):
            square = fold(hacc[k])
            hpart[first + i] = square[:, :BLOCK] + square[:, BLOCK:]
        for d in range(1, n_slab):
            spread(group, d).start()

    def reduce_sums(group):
        first, ks = slots[group]
        mine_rows = pl.ds(pl.multiple_of(mine * rows, rows), rows)
        piece = hpart[first : first + len(ks), mine_rows, :]
        for d in range(1, n_slab):
            spread(group, d).wait_recv()
            piece += hin[d, first : first + len(ks)]
        hsum[first : first + len(ks), mine_rows, :] = piece
        for d in range(1, n_slab):
            share(group, d).start()

    volume = 1.0 / math.sqrt(SEG)

    def finish_sums(group):
        first, ks = slots[group]
        for d in range(1, n_slab):
            share(group, d).wait_recv()
        for i, k in enumerate(ks):
            high, low = split_rows(hsum[first + i] * (-volume * listed(k)))
            both = lax.dot_general(
                sorter[1, :, :BLOCK], jnp.concatenate([high, low], axis=1),
                (((0,), (0,)), ((), ())), preferred_element_type=jnp.float32,
            ).astype(jnp.bfloat16)
            for j in range(2):
                mats[k, 0, :BLOCK, j * BLOCK : (j + 1) * BLOCK] = both[:, :BLOCK]
                mats[k, 0, BLOCK:, j * BLOCK : (j + 1) * BLOCK] = both[:, BLOCK:]

    def times(k, m, stack):
        return fold(jnp.dot(mats[k, m], stack, preferred_element_type=jnp.float32))

    pl.when(mine < n_slab - 1)(
        lambda: pl.semaphore_wait(peers_sem, n_slab - 1 - mine)
    )
    reduce_terms(0)

    @pl.when(is_source)
    def _():
        pl.semaphore_wait(ready_sem, 1)
        detour().start()

    def split_got(m, side, q):
        high, low = split_rows(got[m, side, q])
        got_b[m, side, q, :BLOCK, :] = high
        got_b[m, side, q, BLOCK:, :] = low

    def third_step(q, carry):
        if_goes(LEFT, lambda: start(send(0, LEFT, q)))
        straight = jnp.logical_not(jnp.logical_and(is_source, q == VIA))
        pl.when(jnp.logical_and(has_after, straight))(
            lambda: start(send(0, RIGHT, q))
        )
        for side in (LEFT, RIGHT):
            if_comes(side, lambda: take(send(1, side, q)))

        @pl.when(jnp.logical_and(is_relay, q == VIA - 1))
        def _():
            for i in range(flows):
                if i != far:
                    arrived(i).wait_recv()
                    onward(i).start()

        if far > 0:

            @pl.when(jnp.logical_and(is_stop, q == VIA - 2))
            def _():
                arrived(far).wait_recv()
                second_hop().start()

            @pl.when(jnp.logical_and(is_relay, q == VIA))
            def _():
                arrived(far).wait_recv()
                onward(far).start()

        for side in (LEFT, RIGHT):
            split_got(1, side, q)
            hacc[2 - 2 * side] += across(own_b[0, 1 - side, q], got_b[1, side, q])
            total[1 - side, q] = times(2 - 2 * side, 1, got_b[1, side, q])
        pl.when(q == 1)(lambda: reduce_sums(0))
        return carry

    lax.fori_loop(0, QUARTERS, third_step, 0)

    reduce_terms(1)
    finish_sums(0)

    def own_step(q, carry):
        for side in (LEFT, RIGHT):
            total[side, q] += times(1, 0, own_b[0, side, q])
        return carry

    lax.fori_loop(0, QUARTERS, own_step, 0)
    reduce_sums(1)

    def kernel_step(q, carry):
        for side in (LEFT, RIGHT):
            total[side, q] += times(1, 1, own_b[1, side, q])
        return carry

    lax.fori_loop(0, QUARTERS, kernel_step, 0)
    finish_sums(1)

    def take_last(side, q):
        if side == LEFT:
            if_comes(LEFT, lambda: take(send(0, LEFT, q)))
        else:
            around = jnp.logical_and(is_target, q == VIA)
            pl.when(around)(lambda: whole().wait_recv())
            pl.when(jnp.logical_and(has_before, jnp.logical_not(around)))(
                lambda: take(send(0, RIGHT, q))
            )

    def last_step(q, carry):
        sums = []
        for side in (LEFT, RIGHT):
            take_last(1 - side, q)
            split_got(0, 1 - side, q)
            sums.append(total[side, q] + times(2 * side, 0, got_b[0, 1 - side, q]))
        halves = [
            sums[side][:, t * 128 : (t + 1) * 128]
            for side in (LEFT, RIGHT)
            for t in range(TILES)
        ]
        for i, tile in enumerate(pick(halves, shift[...], lane)):
            at = pl.multiple_of(q * CHUNK_IN + i * 128, 128)
            out_ref[:, pl.ds(at, 128)] = tile
        return carry

    lax.fori_loop(0, QUARTERS, last_step, 0)

    @pl.when(is_relay)
    def _():
        for i in range(flows):
            onward(i).wait_send()

    if far > 0:
        pl.when(is_stop)(lambda: second_hop().wait_send())

    for group in range(2):
        for d in range(1, n_slab):
            spread(group, d).wait_send()
            share(group, d).wait_send()
    for q in range(QUARTERS):
        for m in range(2):
            if_goes(LEFT, lambda: drain(send(m, LEFT, q)))
            if (m, q) == (0, VIA):
                pl.when(is_source)(lambda: whole().wait_send())
                pl.when(jnp.logical_and(has_after, jnp.logical_not(is_source)))(
                    lambda: drain(send(m, RIGHT, q))
                )
            else:
                if_goes(RIGHT, lambda: drain(send(m, RIGHT, q)))


def per_device(n_orb, n_slab, orbitals, offsets, pairs, kernel):
    f32, b16 = jnp.float32, jnp.bfloat16
    dma = pltpu.SemaphoreType.DMA
    hbm = pl.BlockSpec(memory_space=pltpu.HBM)
    vmem = pl.BlockSpec(memory_space=pltpu.VMEM)
    operands = (orbitals, offsets.reshape(n_orb, BLOCK), pairs, kernel)

    def call(most, number):
        return pl.pallas_call(
            functools.partial(body, n_orb, n_slab, most),
            out_shape=(
                pltpu.VMEM((BLOCK, QUARTERS * CHUNK_IN), f32),
                pltpu.SMEM((1, 1), jnp.int32),
            ),
            in_specs=[hbm] * 4,
            out_specs=(vmem, pl.BlockSpec(memory_space=pltpu.SMEM)),
            scratch_shapes=[
                pltpu.VMEM((n_orb, BLOCK), jnp.int32),
                pltpu.VMEM(pairs.shape, jnp.int32),
                pltpu.VMEM(kernel.shape, f32),
                pltpu.VMEM((2, QUARTERS, BLOCK, CHUNK_IN), f32),
                pltpu.VMEM((2, 2, QUARTERS, BLOCK, CHUNK), f32),
                pltpu.VMEM((2, 2, QUARTERS, BLOCK, CHUNK), f32),
                pltpu.VMEM((2, 2, QUARTERS, 2 * BLOCK, CHUNK), b16),
                pltpu.VMEM((2, 2, QUARTERS, 2 * BLOCK, CHUNK), b16),
                pltpu.VMEM((BLOCK, BLOCK), jnp.int32),
                pltpu.VMEM((BLOCK, BLOCK), jnp.int32),
                pltpu.VMEM((3, BLOCK, 2 * BLOCK), b16),
                pltpu.VMEM((3, 2 * BLOCK, 2 * BLOCK), f32),
                pltpu.VMEM((3, BLOCK, BLOCK), f32),
                pltpu.VMEM((n_slab, 3, BLOCK // n_slab, BLOCK), f32),
                pltpu.VMEM((3, BLOCK, BLOCK), f32),
                pltpu.VMEM((3, 2, 2 * BLOCK, 2 * BLOCK), b16),
                pltpu.VMEM((2, QUARTERS, BLOCK, CHUNK), f32),
                dma((2, QUARTERS)), dma((2, 2, QUARTERS, 2)), dma((2, 2, QUARTERS, 2)),
                dma((2, n_slab)), dma((2, n_slab)), dma((2, n_slab)), dma((2, n_slab)),
                dma((3,)),
                pltpu.VMEM((n_orb // ROW - 1, BLOCK, CHUNK), f32),
                dma((n_orb // ROW - 1,)), dma((n_orb // ROW - 1,)),
                pltpu.SemaphoreType.REGULAR, pltpu.SemaphoreType.REGULAR,
            ],
            compiler_params=pltpu.CompilerParams(
                collective_id=number, has_side_effects=True,
                vmem_limit_bytes=40 * 2**20,
            ),
            cost_estimate=pl.CostEstimate(
                flops=2400 * 10**6, bytes_accessed=4 * 2**20, transcendentals=0
            ),
        )(*(pltpu.with_memory_space_constraint(x, pltpu.HBM) for x in operands))

    result, over = call(MOST_ROWS, 0)
    return lax.cond(over.reshape(()) > 0, lambda: call(BLOCK, 1)[0], lambda: result)


def solution(mesh):
    n_orb, n_slab = mesh.shape["orb"], mesh.shape["slab"]
    placed = (P(None, "orb", "slab"), P(), P("orb", None), P("orb", None, None, None))
    return jax.shard_map(
        functools.partial(per_device, n_orb, n_slab), mesh=mesh, in_specs=placed,
        out_specs=P("orb", "slab"), check_vma=False,
    )
```

```python
import functools
import math

import jax
import jax.numpy as jnp
from jax import lax
from jax.experimental import pallas as pl
from jax.experimental.pallas import tpu as pltpu
from jax.sharding import PartitionSpec as P

BLOCK = 128
PATCH = 256
SPREAD = 128
BSTEP = 192
SEG = 16384
QUARTERS = 4
PLANES = 2
CHUNK_IN = PLANES * PATCH
TILE = 64
TILES = BSTEP // TILE
CHUNK = PLANES * BSTEP
MOST_ROWS = 88
MESH = pl.DeviceIdType.MESH
LEFT, RIGHT = 0, 1
ROW = 8
VIA = QUARTERS - 1


def lane_gather(tile, index):
    return jnp.take_along_axis(tile, index, axis=1, mode="promise_in_bounds")


def split_rows(value):
    high = value.astype(jnp.bfloat16)
    low = (value - high.astype(jnp.float32)).astype(jnp.bfloat16)
    return high, low


def fold(square):
    return square[:BLOCK] + square[BLOCK:]


def place(planes, u, lane):
    merged = []
    for v in range(2):
        vregs = [planes[:, (2 * x + v) * 128 : (2 * x + v + 1) * 128] for x in range(PLANES)]
        row = []
        for s in range(PLANES):
            turned = [
                lane_gather(vregs[x], jnp.bitwise_and(lane + TILE * (s - x) - u, 127))
                for x in range(PLANES)
            ]
            row.append(jnp.where(lane < TILE, turned[0], turned[1]))
        merged.append(row)
    zero = jnp.zeros_like(merged[0][0])
    within = jnp.bitwise_and(lane, TILE - 1) - u
    left, right = [], []
    for t in range(TILES):
        at = within + TILE * t
        near, far = merged[0][t % 2], merged[1][t % 2]
        left.append(jnp.where(at < 0, zero, jnp.where(at < 128, near, far)))
        at = within + TILE * t + BSTEP
        near, far = merged[0][(t + 1) % 2], merged[1][(t + 1) % 2]
        right.append(jnp.where(at < 128, near, jnp.where(at < 256, far, zero)))
    return left, right


def pick(tiles, u, lane):
    column = lane + u
    outs = []
    for x in range(PLANES):
        index = jnp.bitwise_and(column, TILE - 1) + TILE * x
        turned = [lane_gather(tile, index) for tile in tiles]
        for first in (0, 2):
            value = turned[first + 3]
            for t in range(2, -1, -1):
                value = jnp.where(column < TILE * (t + 1), turned[first + t], value)
            outs.append(value)
    return outs


def pieces(side, most):
    if most == BLOCK:
        return ((0, BLOCK, 0, CHUNK),)
    if side == LEFT:
        return ((0, BLOCK, 128, CHUNK), (0, most, 0, 128))
    return ((0, BLOCK, 0, CHUNK - 128), (BLOCK - most, BLOCK, CHUNK - 128, CHUNK))


def body(
    n_orb, n_slab, most, orb_hbm, off_hbm, pairs_hbm, ker_hbm, out_ref, over_ref,
    off_ref, pairs_ref, ker_ref, x_in, own, got, own_b, got_b, shift, sorted_shift, sorter, hacc, hpart, hin, hsum, mats, total,
    in_sem, send_sem, recv_sem, rs_send, rs_recv, ag_send, ag_recv, small_sem,
    held, held_sem, onward_sem, ready_sem, peers_sem,
):
    me = lax.axis_index("orb")
    mine = lax.axis_index("slab")
    has_before = me > 0
    has_after = me < n_orb - 1
    before = jnp.maximum(me - 1, 0)
    after = jnp.minimum(me + 1, n_orb - 1)
    rows = BLOCK // n_slab

    flows = n_orb // ROW - 1
    last = n_orb - 1
    flow_end = lax.rem(me, ROW) == ROW - 1
    is_source = jnp.logical_and(flow_end, me < last)
    is_relay = me == last
    is_target = jnp.logical_and(lax.rem(me, ROW) == 0, me > 0)
    flow = me // ROW
    far = 1 if flows >= 3 else -1
    stop = (far + 1) * ROW + ROW - 1 if flows >= 3 else last
    is_stop = jnp.logical_and(me == stop, stop < last)
    via = jnp.where(flow == far, stop, last)

    def detour():
        return pltpu.make_async_remote_copy(
            src_ref=own.at[0, RIGHT, VIA], dst_ref=held.at[flow],
            send_sem=send_sem.at[0, RIGHT, VIA, 0], recv_sem=held_sem.at[flow],
            device_id=(via, mine), device_id_type=MESH,
        )

    def onward(i):
        return pltpu.make_async_remote_copy(
            src_ref=held.at[i], dst_ref=got.at[0, RIGHT, VIA],
            send_sem=onward_sem.at[i], recv_sem=recv_sem.at[0, RIGHT, VIA, 0],
            device_id=((i + 1) * ROW, mine), device_id_type=MESH,
        )

    def second_hop():
        return pltpu.make_async_remote_copy(
            src_ref=held.at[far], dst_ref=held.at[far],
            send_sem=onward_sem.at[far], recv_sem=held_sem.at[far],
            device_id=(last, mine), device_id_type=MESH,
        )

    def arrived(i):
        return pltpu.make_async_remote_copy(
            src_ref=held.at[i], dst_ref=held.at[i],
            send_sem=onward_sem.at[i], recv_sem=held_sem.at[i],
            device_id=(before, mine), device_id_type=MESH,
        )

    def load(m, q):
        return pltpu.make_async_copy(
            orb_hbm.at[m, :, pl.ds(pl.multiple_of(q * CHUNK_IN, CHUNK_IN), CHUNK_IN)],
            x_in.at[m, q], in_sem.at[m, q],
        )

    def send(m, side, q):
        copies = []
        for i, (top, bottom, first, end) in enumerate(pieces(side, most)):
            src, dst = (
                ref.at[m, side, q, top:bottom, first:end] for ref in (own, got)
            )
            copies.append(
                pltpu.make_async_remote_copy(
                    src_ref=src, dst_ref=dst,
                    send_sem=send_sem.at[m, side, q, i],
                    recv_sem=recv_sem.at[m, side, q, i],
                    device_id=(before if side == LEFT else after, mine),
                    device_id_type=MESH,
                )
            )
        return copies

    def whole():
        return pltpu.make_async_remote_copy(
            src_ref=own.at[0, RIGHT, VIA], dst_ref=got.at[0, RIGHT, VIA],
            send_sem=send_sem.at[0, RIGHT, VIA, 0],
            recv_sem=recv_sem.at[0, RIGHT, VIA, 0],
            device_id=(before, mine), device_id_type=MESH,
        )

    def start(copies):
        for copy in copies:
            copy.start()

    def take(copies):
        for copy in copies:
            copy.wait_recv()

    def drain(copies):
        for copy in copies:
            copy.wait_send()

    def if_goes(side, action):
        pl.when(has_before if side == LEFT else has_after)(action)

    def if_comes(side, action):
        pl.when(has_after if side == LEFT else has_before)(action)

    small = [
        pltpu.make_async_copy(src, dst, small_sem.at[i])
        for i, (src, dst) in enumerate(
            ((off_hbm, off_ref), (pairs_hbm, pairs_ref), (ker_hbm, ker_ref))
        )
    ]
    barrier = pltpu.get_barrier_semaphore()

    def greet(device):
        pl.semaphore_signal(barrier, inc=1, device_id=device, device_id_type=MESH)

    small[0].start()
    load(1, 0).start()
    if_goes(LEFT, lambda: greet((before, mine)))
    if_goes(RIGHT, lambda: greet((after, mine)))
    pl.when(is_source)(lambda: greet((via, mine)))
    pl.when(is_target)(lambda: greet((last, mine)))
    for d in range(1, n_slab):
        peer = lax.rem(mine + d, n_slab)
        pl.when(peer > mine)(lambda: greet((me, peer)))
    for q in range(1, QUARTERS):
        load(1, q).start()
    for q in range(QUARTERS):
        load(0, q).start()
    small[1].start()
    small[2].start()

    small[0].wait()
    lane = lax.broadcasted_iota(jnp.int32, (BLOCK, BLOCK), 1)
    line = lax.broadcasted_iota(jnp.int32, (BLOCK, BLOCK), 0)

    def shifts_of(block):
        across_lanes = jnp.broadcast_to(
            off_ref[pl.ds(block, 1), :] - BSTEP * block, (BLOCK, BLOCK)
        )
        return across_lanes, jnp.transpose(across_lanes)

    def sorter_of(across_lanes, down_rows):
        ahead = (down_rows < across_lanes) | ((down_rows == across_lanes) & (line < lane))
        place_of = jnp.sum(ahead.astype(jnp.float32), axis=0, keepdims=True)
        return (place_of == line.astype(jnp.float32)).astype(jnp.float32)

    across_lanes, down_rows = shifts_of(me)
    shift[...] = down_rows
    one_hot = sorter_of(across_lanes, down_rows)
    sorter[1, :, :BLOCK] = one_hot.astype(jnp.bfloat16)
    sorter[1, :, BLOCK:] = one_hot.astype(jnp.bfloat16)
    sorted_shift[...] = jnp.dot(
        sorter[1, :, :BLOCK], down_rows.astype(jnp.float32).astype(jnp.bfloat16),
        preferred_element_type=jnp.float32,
    ).astype(jnp.int32)

    def place_chunk(m, q):
        high, low = split_rows(x_in[m, q])
        planes = jnp.dot(
            sorter[1], jnp.concatenate([high, low], axis=0),
            preferred_element_type=jnp.float32,
        )
        left, right = place(planes, sorted_shift[...], lane)
        for side, tiles in ((LEFT, left), (RIGHT, right)):
            for i, tile in enumerate(tiles):
                own[m, side, q, :, i * 128 : (i + 1) * 128] = tile

    def split_own(m, q):
        for side in (LEFT, RIGHT):
            high, low = split_rows(own[m, side, q])
            own_b[m, side, q, :BLOCK, :] = high
            own_b[m, side, q, BLOCK:, :] = low

    def send_both(m, q):
        if_goes(LEFT, lambda: start(send(m, LEFT, q)))
        if_goes(RIGHT, lambda: start(send(m, RIGHT, q)))

    load(1, 0).wait()
    place_chunk(1, 0)
    pl.semaphore_wait(
        barrier,
        mine + has_before.astype(jnp.int32) + has_after.astype(jnp.int32)
        + (2 * flows - (far > 0)) * is_relay.astype(jnp.int32)
        + is_stop.astype(jnp.int32),
    )

    def ready(i):
        pl.semaphore_signal(
            ready_sem, inc=1, device_id=(i * ROW + ROW - 1, mine), device_id_type=MESH
        )


    @pl.when(is_relay)
    def _():
        for i in range(flows):
            if i != far:
                ready(i)

    if far > 0:
        pl.when(is_stop)(lambda: ready(far))

    send_both(1, 0)

    for d in range(1, n_slab):
        peer = lax.rem(mine + d, n_slab)

        @pl.when(peer < mine)
        def _():
            pl.semaphore_signal(
                peers_sem, inc=1, device_id=(me, peer), device_id_type=MESH
            )

    def first_step(q, carry):
        load(1, q).wait()
        place_chunk(1, q)
        send_both(1, q)
        return carry

    lax.fori_loop(1, QUARTERS, first_step, 0)

    def blank(q, carry):
        for side in (LEFT, RIGHT):
            comes = has_after if side == LEFT else has_before

            @pl.when(jnp.logical_not(comes))
            def _():
                for m in range(2):
                    got[m, side, q] = jnp.zeros((BLOCK, CHUNK), jnp.float32)

            if most < BLOCK:

                @pl.when(comes)
                def _():
                    for m in range(2):
                        gap = jnp.zeros((BLOCK - most, 128), jnp.float32)
                        if side == LEFT:
                            got[m, side, q, most:, :128] = gap
                        elif m == 1:
                            got[m, side, q, : BLOCK - most, CHUNK - 128 :] = gap
                        else:

                            @pl.when(jnp.logical_not(is_target & (q == VIA)))
                            def _():
                                got[0, side, q, : BLOCK - most, CHUNK - 128 :] = gap

        return carry

    def other_sorters():
        for k, block in ((0, before), (2, after)):
            sorter[k, :, :BLOCK] = sorter_of(*shifts_of(block)).astype(jnp.bfloat16)

    windows = off_ref[...] - BSTEP * lax.broadcasted_iota(jnp.int32, (n_orb, BLOCK), 0)
    excess = jnp.zeros((n_orb, 1), jnp.float32)
    for inside in (windows < TILE, windows > SPREAD - TILE):
        count = jnp.sum(inside.astype(jnp.float32), axis=1, keepdims=True)
        excess = jnp.maximum(excess, count - most)
    over_ref[0, 0] = jnp.max(excess).astype(jnp.int32)

    lax.fori_loop(0, QUARTERS, blank, 0)
    other_sorters()
    small[1].wait()
    small[2].wait()

    def across(a, b):
        return lax.dot_general(
            a, b, (((1,), (1,)), ((), ())), preferred_element_type=jnp.float32
        )

    def listed(k):
        return jnp.broadcast_to(
            pairs_ref[0:1, k : k + 1].astype(jnp.float32), (BLOCK, BLOCK)
        )

    for k in range(3):
        high, low = split_rows(ker_ref[0, k] * listed(k))
        both = across(jnp.concatenate([high, low], axis=0), sorter[k, :, :BLOCK])
        for j in range(2):
            mats[k, 1, :, j * BLOCK : (j + 1) * BLOCK] = both.astype(jnp.bfloat16)
        hacc[k] = jnp.zeros((2 * BLOCK, 2 * BLOCK), jnp.float32)

    def second_step(q, carry):
        load(0, q).wait()
        place_chunk(0, q)
        split_own(1, q)
        split_own(0, q)
        for side in (LEFT, RIGHT):
            hacc[1] += across(own_b[0, side, q], own_b[1, side, q])
        return carry

    lax.fori_loop(0, QUARTERS, second_step, 0)

    slots = ((2, (1,)), (0, (0, 2)))

    def spread(group, d):
        first, ks = slots[group]
        peer = lax.rem(mine + d, n_slab)
        there = pl.ds(pl.multiple_of(peer * rows, rows), rows)
        return pltpu.make_async_remote_copy(
            src_ref=hpart.at[first : first + len(ks), there, :],
            dst_ref=hin.at[d, first : first + len(ks)],
            send_sem=rs_send.at[group, d], recv_sem=rs_recv.at[group, d],
            device_id=(me, peer), device_id_type=MESH,
        )

    def share(group, d):
        first, ks = slots[group]
        peer = lax.rem(mine + d, n_slab)
        here = pl.ds(pl.multiple_of(mine * rows, rows), rows)
        part = hsum.at[first : first + len(ks), here, :]
        return pltpu.make_async_remote_copy(
            src_ref=part, dst_ref=part,
            send_sem=ag_send.at[group, d], recv_sem=ag_recv.at[group, d],
            device_id=(me, peer), device_id_type=MESH,
        )

    def reduce_terms(group):
        first, ks = slots[group]
        for i, k in enumerate(ks):
            square = fold(hacc[k])
            hpart[first + i] = square[:, :BLOCK] + square[:, BLOCK:]
        for d in range(1, n_slab):
            spread(group, d).start()

    def reduce_sums(group):
        first, ks = slots[group]
        mine_rows = pl.ds(pl.multiple_of(mine * rows, rows), rows)
        piece = hpart[first : first + len(ks), mine_rows, :]
        for d in range(1, n_slab):
            spread(group, d).wait_recv()
            piece += hin[d, first : first + len(ks)]
        hsum[first : first + len(ks), mine_rows, :] = piece
        for d in range(1, n_slab):
            share(group, d).start()

    volume = 1.0 / math.sqrt(SEG)

    def finish_sums(group):
        first, ks = slots[group]
        for d in range(1, n_slab):
            share(group, d).wait_recv()
        for i, k in enumerate(ks):
            high, low = split_rows(hsum[first + i] * (-volume * listed(k)))
            both = lax.dot_general(
                sorter[1, :, :BLOCK], jnp.concatenate([high, low], axis=1),
                (((0,), (0,)), ((), ())), preferred_element_type=jnp.float32,
            ).astype(jnp.bfloat16)
            for j in range(2):
                mats[k, 0, :BLOCK, j * BLOCK : (j + 1) * BLOCK] = both[:, :BLOCK]
                mats[k, 0, BLOCK:, j * BLOCK : (j + 1) * BLOCK] = both[:, BLOCK:]

    def times(k, m, stack):
        return fold(jnp.dot(mats[k, m], stack, preferred_element_type=jnp.float32))

    pl.when(mine < n_slab - 1)(
        lambda: pl.semaphore_wait(peers_sem, n_slab - 1 - mine)
    )
    reduce_terms(0)

    @pl.when(is_source)
    def _():
        pl.semaphore_wait(ready_sem, 1)
        detour().start()

    def split_got(m, side, q):
        high, low = split_rows(got[m, side, q])
        got_b[m, side, q, :BLOCK, :] = high
        got_b[m, side, q, BLOCK:, :] = low

    def third_step(q, carry):
        for side in (LEFT, RIGHT):
            if_comes(side, lambda: take(send(1, side, q)))
        if_goes(LEFT, lambda: start(send(0, LEFT, q)))
        straight = jnp.logical_not(jnp.logical_and(is_source, q == VIA))
        pl.when(jnp.logical_and(has_after, straight))(
            lambda: start(send(0, RIGHT, q))
        )

        @pl.when(jnp.logical_and(is_relay, q == VIA - 1))
        def _():
            for i in range(flows):
                if i != far:
                    arrived(i).wait_recv()
                    onward(i).start()

        if far > 0:

            @pl.when(jnp.logical_and(is_stop, q == VIA - 2))
            def _():
                arrived(far).wait_recv()
                second_hop().start()

            @pl.when(jnp.logical_and(is_relay, q == VIA))
            def _():
                arrived(far).wait_recv()
                onward(far).start()

        for side in (LEFT, RIGHT):
            split_got(1, side, q)
            hacc[2 - 2 * side] += across(own_b[0, 1 - side, q], got_b[1, side, q])
            total[1 - side, q] = times(2 - 2 * side, 1, got_b[1, side, q])
        pl.when(q == 1)(lambda: reduce_sums(0))
        return carry

    lax.fori_loop(0, QUARTERS, third_step, 0)

    reduce_terms(1)
    finish_sums(0)

    def own_step(q, carry):
        for side in (LEFT, RIGHT):
            total[side, q] += times(1, 0, own_b[0, side, q])
        return carry

    lax.fori_loop(0, QUARTERS, own_step, 0)
    reduce_sums(1)

    def kernel_step(q, carry):
        for side in (LEFT, RIGHT):
            total[side, q] += times(1, 1, own_b[1, side, q])
        return carry

    lax.fori_loop(0, QUARTERS, kernel_step, 0)
    finish_sums(1)

    def take_last(side, q):
        if side == LEFT:
            if_comes(LEFT, lambda: take(send(0, LEFT, q)))
        else:
            around = jnp.logical_and(is_target, q == VIA)
            pl.when(around)(lambda: whole().wait_recv())
            pl.when(jnp.logical_and(has_before, jnp.logical_not(around)))(
                lambda: take(send(0, RIGHT, q))
            )

    def last_step(q, carry):
        sums = []
        for side in (LEFT, RIGHT):
            take_last(1 - side, q)
            split_got(0, 1 - side, q)
            sums.append(total[side, q] + times(2 * side, 0, got_b[0, 1 - side, q]))
        halves = [
            sums[side][:, t * 128 : (t + 1) * 128]
            for side in (LEFT, RIGHT)
            for t in range(TILES)
        ]
        for i, tile in enumerate(pick(halves, shift[...], lane)):
            at = pl.multiple_of(q * CHUNK_IN + i * 128, 128)
            out_ref[:, pl.ds(at, 128)] = tile
        return carry

    lax.fori_loop(0, QUARTERS, last_step, 0)

    @pl.when(is_relay)
    def _():
        for i in range(flows):
            onward(i).wait_send()

    if far > 0:
        pl.when(is_stop)(lambda: second_hop().wait_send())

    for group in range(2):
        for d in range(1, n_slab):
            spread(group, d).wait_send()
            share(group, d).wait_send()
    for q in range(QUARTERS):
        for m in range(2):
            if_goes(LEFT, lambda: drain(send(m, LEFT, q)))
            if (m, q) == (0, VIA):
                pl.when(is_source)(lambda: whole().wait_send())
                pl.when(jnp.logical_and(has_after, jnp.logical_not(is_source)))(
                    lambda: drain(send(m, RIGHT, q))
                )
            else:
                if_goes(RIGHT, lambda: drain(send(m, RIGHT, q)))


def per_device(n_orb, n_slab, orbitals, offsets, pairs, kernel):
    f32, b16 = jnp.float32, jnp.bfloat16
    dma = pltpu.SemaphoreType.DMA
    hbm = pl.BlockSpec(memory_space=pltpu.HBM)
    vmem = pl.BlockSpec(memory_space=pltpu.VMEM)
    operands = (orbitals, offsets.reshape(n_orb, BLOCK), pairs, kernel)

    def call(most, number):
        return pl.pallas_call(
            functools.partial(body, n_orb, n_slab, most),
            out_shape=(
                pltpu.VMEM((BLOCK, QUARTERS * CHUNK_IN), f32),
                pltpu.SMEM((1, 1), jnp.int32),
            ),
            in_specs=[hbm] * 4,
            out_specs=(vmem, pl.BlockSpec(memory_space=pltpu.SMEM)),
            scratch_shapes=[
                pltpu.VMEM((n_orb, BLOCK), jnp.int32),
                pltpu.VMEM(pairs.shape, jnp.int32),
                pltpu.VMEM(kernel.shape, f32),
                pltpu.VMEM((2, QUARTERS, BLOCK, CHUNK_IN), f32),
                pltpu.VMEM((2, 2, QUARTERS, BLOCK, CHUNK), f32),
                pltpu.VMEM((2, 2, QUARTERS, BLOCK, CHUNK), f32),
                pltpu.VMEM((2, 2, QUARTERS, 2 * BLOCK, CHUNK), b16),
                pltpu.VMEM((2, 2, QUARTERS, 2 * BLOCK, CHUNK), b16),
                pltpu.VMEM((BLOCK, BLOCK), jnp.int32),
                pltpu.VMEM((BLOCK, BLOCK), jnp.int32),
                pltpu.VMEM((3, BLOCK, 2 * BLOCK), b16),
                pltpu.VMEM((3, 2 * BLOCK, 2 * BLOCK), f32),
                pltpu.VMEM((3, BLOCK, BLOCK), f32),
                pltpu.VMEM((n_slab, 3, BLOCK // n_slab, BLOCK), f32),
                pltpu.VMEM((3, BLOCK, BLOCK), f32),
                pltpu.VMEM((3, 2, 2 * BLOCK, 2 * BLOCK), b16),
                pltpu.VMEM((2, QUARTERS, BLOCK, CHUNK), f32),
                dma((2, QUARTERS)), dma((2, 2, QUARTERS, 2)), dma((2, 2, QUARTERS, 2)),
                dma((2, n_slab)), dma((2, n_slab)), dma((2, n_slab)), dma((2, n_slab)),
                dma((3,)),
                pltpu.VMEM((n_orb // ROW - 1, BLOCK, CHUNK), f32),
                dma((n_orb // ROW - 1,)), dma((n_orb // ROW - 1,)),
                pltpu.SemaphoreType.REGULAR, pltpu.SemaphoreType.REGULAR,
            ],
            compiler_params=pltpu.CompilerParams(
                collective_id=number, has_side_effects=True,
                vmem_limit_bytes=40 * 2**20,
            ),
            cost_estimate=pl.CostEstimate(
                flops=2400 * 10**6, bytes_accessed=4 * 2**20, transcendentals=0
            ),
        )(*(pltpu.with_memory_space_constraint(x, pltpu.HBM) for x in operands))

    result, over = call(MOST_ROWS, 0)
    return lax.cond(over.reshape(()) > 0, lambda: call(BLOCK, 1)[0], lambda: result)


def solution(mesh):
    n_orb, n_slab = mesh.shape["orb"], mesh.shape["slab"]
    placed = (P(None, "orb", "slab"), P(), P("orb", None), P("orb", None, None, None))
    return jax.shard_map(
        functools.partial(per_device, n_orb, n_slab), mesh=mesh, in_specs=placed,
        out_specs=P("orb", "slab"), check_vma=False,
    )
```
